32 devices in a mesh: stations: 4 (over z), tm: 8 (over y, x, core).
Axes of the slice: x: 2, y: 2, z: 4, core: 2. Of those that a mesh axis runs over, the one named last changes fastest.
Arguments:
- patch_embedding_tensor: bfloat16 [16, 1024, 512], P('stations', 'tm'), may hold values from -6 to 6
- qkv_projector_matrix: bfloat16 [512, 1536], replicated, may hold values from -0.25 to 0.25
- closing_projector_matrix: bfloat16 [1024, 512], replicated, may hold values from -0.1875 to 0.1875
- logit_sharpness: float32 [8], replicated, may hold values from 0.5 to 2
- adjacent_group_table: int32 [16, 8], P('stations'), may hold values from 0 to 15, as said below
- adjacent_valid_tally: int32 [16], P('stations'), may hold values from 1 to 8
Outputs:
- encoded: bfloat16 [16, 1024, 512], P('stations', 'tm')
The draws below stay inside these ranges and needn't reach their ends.
Inputs may be any that keep to these rules, and one draw needn't show every extreme that they name: `adjacent_group_table`: slot 0 of row g names g itself; every entry of row g lies within 4 of g.
All inputs are finite; a program needn't handle non-finite values.
Results may differ from the reference program's by a relative error of at most 0.0062.
Values may be sent and summed in bfloat16 or wider, within the bound.
No kernel may reach another device: no remote copies, remote signals or barrier semaphores. Data moves between devices by JAX's collectives and lax.ppermute only.
A program may use at most 128 MiB of HBM per device.

```python
import math
import jax
import jax.numpy as jnp
from jax import lax

D = 512
FOCUS_CHANNELS = 8
NB = 8
NEAR = 4
P_DEV = 128
G = 16
P_SIZE = 1024


def draw_adjacent_group_table(key, part):
    groups = jnp.arange(G, dtype=jnp.int32)
    choices_all = 2 * NEAR
    ranking = jax.random.randint(key, (G, choices_all), 0, 1 << 20) * choices_all + jnp.arange(choices_all, dtype=jnp.int32)[None, :]
    ordering = jnp.argsort(ranking, axis=1).astype(jnp.int32)
    offset = jnp.where(ordering < NEAR, ordering - NEAR, ordering - NEAR + 1)[:, :NB - 1]
    target = groups[:, None] + offset
    inside = (target >= 0) & (target < G)
    target = jnp.where(inside, target, groups[:, None] + jnp.zeros_like(target))
    return jnp.concatenate([groups[:, None], target], axis=1).astype(jnp.int32)


def draw_adjacent_valid_tally(key, part):
    counts = jax.random.randint(key, (G,), 1, NB + 1).astype(jnp.int32)
    return counts.at[0].set(NB).at[G - 1].set(1)


def steps_of(stream_key, extent, shards, smallest, top_value):
    level = 1.0
    for axis_at, shards_of in shards:
        heights = jax.random.uniform(jax.random.fold_in(jax.random.fold_in(stream_key, 6), axis_at), (shards_of,), jnp.float32, smallest / len(shards), top_value / len(shards))
        level = level * jnp.repeat(jnp.exp(heights), extent[axis_at] // shards_of).reshape((-1,) + (1,) * (len(extent) - 1 - axis_at))
    return level


def bell_draw(rng, shape, width, most, pieces=(), kind=jnp.bfloat16):
    values = width * jax.random.normal(rng, shape, jnp.float32)
    if pieces:
        values = values * steps_of(rng, shape, pieces, -0.22, 0.18)
    return jnp.clip(values, -most, most).astype(kind)


def setup_inputs(seed: int = 0) -> dict:
    seeds = jax.random.split(jax.random.key(seed), 7)
    return {
        "patch_embedding_tensor": bell_draw(seeds[0], (G, P_SIZE, D), 1.0, 6.0, ((0, 4), (1, 8))),
        "qkv_projector_matrix": bell_draw(seeds[1], (D, 3 * D), D ** -0.5, 0.25),
        "closing_projector_matrix": bell_draw(seeds[2], (2 * D, D), (2 * D) ** -0.5, 0.1875),
        "logit_sharpness": jnp.clip(jax.random.uniform(seeds[3], (FOCUS_CHANNELS,), jnp.float32, 0.5, 2.0), 0.5, 2.0),
        "adjacent_group_table": draw_adjacent_group_table(jax.random.fold_in(seeds[6], 71), 0),
        "adjacent_valid_tally": draw_adjacent_valid_tally(jax.random.fold_in(seeds[6], 71), 0),
    }


def head_norm(values, epsilon):
    return values * lax.rsqrt(lax.optimization_barrier(jnp.mean(values * values, axis=-1, keepdims=True)) + epsilon)

def keys_values(normed, weight_cols, channel_tally):
    group_count, patch_count, model_width = normed.shape
    channel_breadth = model_width // channel_tally
    projected = jnp.dot(normed.reshape(-1, model_width), weight_cols, preferred_element_type=jnp.float32)
    projected = projected.reshape(group_count, patch_count, 2, channel_tally, channel_breadth)
    key_rows = head_norm(projected[:, :, 0], 1e-06).astype(jnp.bfloat16)
    value_rows = projected[:, :, 1].astype(jnp.bfloat16)
    return (key_rows, value_rows)

def reference(patch_embedding_tensor, qkv_projector_matrix, closing_projector_matrix, logit_sharpness, adjacent_group_table, adjacent_valid_tally):
    group_count, patch_total, model_width = patch_embedding_tensor.shape
    channel_tally = logit_sharpness.shape[0]
    channel_breadth = model_width // channel_tally
    group_ids = jnp.arange(group_count, dtype=jnp.int32)
    live_slots = jnp.arange(adjacent_group_table.shape[1], dtype=jnp.int32)[None, :] < adjacent_valid_tally[:, None]
    matches = (adjacent_group_table[:, :, None] == group_ids[None, None, :]) & live_slots[:, :, None]
    multiplicity = lax.optimization_barrier(jnp.sum(matches.astype(jnp.int32), axis=1)).astype(jnp.float32)
    blocks = patch_embedding_tensor.reshape(group_count, patch_total // P_DEV, P_DEV, model_width).transpose(1, 0, 2, 3)
    positions = jnp.arange(P_DEV, dtype=jnp.int32)
    causal = positions[:, None] >= positions[None, :]
    highest = lax.Precision.HIGHEST

    def advance(carried, block):
        inputs_f = block.astype(jnp.float32)
        normed = head_norm(inputs_f, 1e-06).astype(jnp.bfloat16)
        queries_f = jnp.dot(normed.reshape(-1, model_width), qkv_projector_matrix[:, :model_width], preferred_element_type=jnp.float32)
        queries = head_norm(queries_f.reshape(group_count, P_DEV, channel_tally, channel_breadth), 1e-06).astype(jnp.bfloat16)
        key_rows, value_rows = keys_values(normed, qkv_projector_matrix[:, model_width:], channel_tally)
        queries_w = queries.astype(jnp.float32)
        keys_w = key_rows.astype(jnp.float32)
        values_w = value_rows.astype(jnp.float32)
        scores_time = jnp.einsum('gthd,gshd->ghts', queries_w, keys_w, precision=highest)
        scores_time = jnp.where(causal[None, None], scores_time, jnp.zeros_like(scores_time))
        scores_time = scores_time.astype(jnp.bfloat16).astype(jnp.float32)
        local_part = jnp.einsum('ghts,gshd->gthd', scores_time, values_w, precision=highest)
        prefix_states = carried.astype(jnp.bfloat16).astype(jnp.float32)
        linear_sum = local_part + jnp.einsum('gthd,ghde->gthe', queries_w, prefix_states, precision=highest)
        states = jnp.einsum('gthd,gthe->ghde', keys_w, values_w, precision=highest)
        linear_out = head_norm(linear_sum, 1e-05).astype(jnp.bfloat16)
        affinity_logits = jnp.einsum('gthd,nthd->gthn', queries_w, keys_w, precision=highest)
        affinity_logits = affinity_logits * (logit_sharpness[None, None, :, None] / math.sqrt(channel_breadth))
        exponent = multiplicity[:, None, None, :] * jnp.exp(affinity_logits)
        weights = (exponent / lax.optimization_barrier(jnp.sum(exponent, axis=-1, keepdims=True))).astype(jnp.bfloat16)
        gathered = jnp.einsum('gthn,nthd->gthd', weights.astype(jnp.float32), values_w, precision=highest).astype(jnp.bfloat16)
        joined = jnp.concatenate([linear_out.reshape(group_count, P_DEV, model_width), gathered.reshape(group_count, P_DEV, model_width)], axis=2)
        mixed = jnp.dot(joined.reshape(-1, 2 * model_width), closing_projector_matrix, preferred_element_type=jnp.float32)
        result = (inputs_f + mixed.reshape(group_count, P_DEV, model_width)).astype(jnp.bfloat16)
        return (carried + states, result)
    start = jnp.zeros((group_count, channel_tally, channel_breadth, channel_breadth), jnp.float32)
    final, outputs = lax.scan(advance, start, blocks)
    return outputs.transpose(1, 0, 2, 3).reshape(group_count, patch_total, model_width)
```

```python
import functools
import math

import jax
import jax.numpy as jnp
from jax import lax
from jax.experimental import pallas as pl
from jax.experimental.pallas import tpu as pltpu
from jax.sharding import PartitionSpec as P

NEAR = 4
HALF = 256
T = 32
F32 = jnp.float32
BF16 = jnp.bfloat16
VMEM = pltpu.VMEM
SMEM = pltpu.SMEM


def dot(a, b):
    return jnp.dot(a, b, preferred_element_type=F32)


def dot_nt(a, b):
    return lax.dot_general(a, b, (((1,), (1,)), ((), ())), preferred_element_type=F32)


def dot_tn(a, b):
    return lax.dot_general(a, b, (((0,), (0,)), ((), ())), preferred_element_type=F32)


def row_norm(x):
    xf = x.astype(F32)
    return (xf * lax.rsqrt(jnp.mean(xf * xf, axis=-1, keepdims=True) + 1e-06)).astype(BF16)


def head_ids(shape, axis, breadth):
    return lax.broadcasted_iota(jnp.int32, shape, axis) // breadth


def mean_matrix(breadth):
    same = head_ids((HALF, HALF), 0, breadth) == head_ids((HALF, HALF), 1, breadth)
    return jnp.where(same, 1.0 / breadth, 0.0).astype(BF16)


def head_norm(values, means, epsilon):
    square = (values * values).astype(BF16)
    return (values * lax.rsqrt(dot(square, means) + epsilon)).astype(BF16)


def own_head(values, j, breadth):
    ids = head_ids(values.shape, 1, breadth)
    return jnp.where(ids == j, values, jnp.zeros_like(values))


def multiplicity_mask(table_ref, tally_ref, base):
    groups, slots = table_ref.shape
    wide = groups * T
    ids = base + lax.broadcasted_iota(jnp.int32, (8, wide), 1) // T
    rows = []
    for g in range(groups):
        total = jnp.zeros((8, wide), F32)
        for j in range(slots):
            total += jnp.where((ids == table_ref[g, j]) & (j < tally_ref[g]), 1.0, 0.0)
        rows.append(jnp.broadcast_to(total[:1], (T, wide)))
    full = jnp.concatenate(rows, axis=0)
    t_row = lax.broadcasted_iota(jnp.int32, (wide, wide), 0) % T
    t_col = lax.broadcasted_iota(jnp.int32, (wide, wide), 1) % T
    return jnp.where(t_row == t_col, full, 0.0)


def neighbour_chunk(q, k, v, mask, sharp, breadth):
    heads = HALF // breadth
    shares = []
    for j in range(heads):
        score = dot_nt(q, own_head(k, j, breadth))
        shares.append((jnp.exp2(score * sharp[j]) * mask).astype(BF16))
    share = jnp.concatenate(shares, axis=1)
    spread = jnp.concatenate([own_head(v, j, breadth) for j in range(heads)], axis=0)
    ones = jnp.concatenate([own_head(jnp.ones_like(v), j, breadth) for j in range(heads)], axis=0)
    return dot(share, spread), dot(share, ones)


def sharpness_of(sharp_ref, first, heads, breadth):
    scale = math.log2(math.e) / math.sqrt(breadth)
    return [sharp_ref[first + j] * scale for j in range(heads)]


def cut(ref, c, h):
    groups = ref.shape[0]
    return ref[:, c * T : (c + 1) * T, h * HALF : (h + 1) * HALF].reshape(groups * T, HALF)


def states_kernel(breadth, x_ref, w_ref, n_ref, k_ref, v_ref, keep_ref, give_ref):
    groups, patches, width = x_ref.shape
    core = lax.axis_index("tm") % 2
    means = mean_matrix(breadth)
    normed = row_norm(x_ref[...].reshape(groups * patches, width))
    n_ref[...] = normed.reshape(n_ref.shape)
    for h in range(width // HALF):
        at = slice(h * HALF, (h + 1) * HALF)
        k = head_norm(dot(normed, w_ref[:, width + h * HALF : width + (h + 1) * HALF]), means, 1e-06)
        v = dot(normed, w_ref[:, 2 * width + h * HALF : 2 * width + (h + 1) * HALF]).astype(BF16)
        k_ref[:, :, at] = k.reshape(groups, patches, HALF)
        v_ref[:, :, at] = v.reshape(groups, patches, HALF)
        states = []
        for g in range(groups):
            rows = slice(g * patches, (g + 1) * patches)
            full = dot_tn(k[rows], v[rows])
            state = jnp.zeros((breadth, HALF), F32)
            for j in range(HALF // breadth):
                state += own_head(full[j * breadth : (j + 1) * breadth], j, breadth)
            states.append(state)

        @pl.when(core == h)
        def _():
            for g in range(groups):
                keep_ref[g] = states[g]

        @pl.when(core != h)
        def _():
            for g in range(groups):
                give_ref[g] = states[g].astype(BF16)


def own_kernel(breadth, n_ref, w_ref, k_ref, v_ref, sharp_ref, table_ref, tally_ref, q_ref, lin_ref, num_ref, den_ref):
    groups, patches, width = n_ref.shape
    heads = HALF // breadth
    means = mean_matrix(breadth)
    normed = n_ref[...].reshape(groups * patches, width)
    causal = lax.broadcasted_iota(jnp.int32, (patches, patches), 0) >= lax.broadcasted_iota(jnp.int32, (patches, patches), 1)
    mask = multiplicity_mask(table_ref, tally_ref, lax.axis_index("stations") * groups)
    for h in range(width // HALF):
        at = slice(h * HALF, (h + 1) * HALF)
        q = head_norm(dot(normed, w_ref[:, at]), means, 1e-06)
        q_ref[:, :, at] = q.reshape(groups, patches, HALF)
        for g in range(groups):
            k, v = k_ref[g, :, at], v_ref[g, :, at]
            qg = q[g * patches : (g + 1) * patches]
            scores = [jnp.where(causal, dot_nt(qg, own_head(k, j, breadth)), 0.0).astype(BF16) for j in range(heads)]
            spread = jnp.concatenate([own_head(v, j, breadth) for j in range(heads)], axis=0)
            lin_ref[g, :, at] = dot(jnp.concatenate(scores, axis=1), spread)
        sharp = sharpness_of(sharp_ref, h * heads, heads, breadth)
        for c in range(patches // T):
            num, den = neighbour_chunk(cut(q_ref, c, h), cut(k_ref, c, h), cut(v_ref, c, h), mask, sharp, breadth)
            span = slice(c * T, (c + 1) * T)
            num_ref[:, span, at] = num.reshape(groups, T, HALF)
            den_ref[:, span, at] = den.reshape(groups, T, HALF)


def halo(breadth, base, x_ref, w_ref, q_ref, sharp_ref, table_ref, tally_ref, num_ref, den_ref, k_ref, v_ref, emit):
    groups, patches, width = x_ref.shape
    heads = HALF // breadth
    means = mean_matrix(breadth)
    normed = row_norm(x_ref[...].reshape(groups * patches, width))
    mask = multiplicity_mask(table_ref, tally_ref, base)
    for h in range(width // HALF):
        at = slice(h * HALF, (h + 1) * HALF)
        k = head_norm(dot(normed, w_ref[:, width + h * HALF : width + (h + 1) * HALF]), means, 1e-06)
        v = dot(normed, w_ref[:, 2 * width + h * HALF : 2 * width + (h + 1) * HALF]).astype(BF16)
        k_ref[...] = k.reshape(groups, patches, HALF)
        v_ref[...] = v.reshape(groups, patches, HALF)
        sharp = sharpness_of(sharp_ref, h * heads, heads, breadth)
        for c in range(patches // T):
            num, den = neighbour_chunk(cut(q_ref, c, h), cut(k_ref, c, 0), cut(v_ref, c, 0), mask, sharp, breadth)
            span = slice(c * T, (c + 1) * T)
            emit(span, at, num.reshape(groups, T, HALF) + num_ref[:, span, at], den.reshape(groups, T, HALF) + den_ref[:, span, at])


def even_kernel(breadth, x_ref, w_ref, q_ref, sharp_ref, table_ref, tally_ref, num_ref, den_ref, num_out, den_out, k_ref, v_ref):
    base = (lax.axis_index("stations") ^ 1) * x_ref.shape[0]

    def emit(span, at, num, den):
        num_out[:, span, at] = num
        den_out[:, span, at] = den

    halo(breadth, base, x_ref, w_ref, q_ref, sharp_ref, table_ref, tally_ref, num_ref, den_ref, k_ref, v_ref, emit)


def odd_kernel(breadth, x_ref, w_ref, q_ref, sharp_ref, table_ref, tally_ref, num_ref, den_ref, own_ref, close_ref, y_ref, k_ref, v_ref, gathered_ref):
    groups, patches, width = x_ref.shape
    station = lax.axis_index("stations")
    base = (station + 2 * (station % 2) - 1) * groups

    def emit(span, at, num, den):
        gathered_ref[:, span, at] = (num / den).astype(BF16)

    halo(breadth, base, x_ref, w_ref, q_ref, sharp_ref, table_ref, tally_ref, num_ref, den_ref, k_ref, v_ref, emit)
    mixed = dot(gathered_ref[...].reshape(groups * patches, width), close_ref[width:, :])
    y_ref[...] = own_ref[...].astype(F32) + mixed.reshape(groups, patches, width)


def closing_kernel(breadth, q_ref, lin_ref, mine_ref, other_ref, close_ref, y_ref, out_ref, normed_ref):
    groups, patches, width = q_ref.shape
    heads = HALF // breadth
    core = lax.axis_index("tm") % 2
    means = mean_matrix(breadth)
    same = head_ids((HALF, HALF), 0, breadth) == head_ids((HALF, HALF), 1, breadth)
    for h in range(width // HALF):
        at = slice(h * HALF, (h + 1) * HALF)
        for g in range(groups):
            state = jnp.where(core == h, mine_ref[g], other_ref[g].astype(F32))
            block = jnp.where(same, jnp.concatenate([state] * heads, axis=0), 0.0).astype(BF16)
            total = lin_ref[g, :, at] + dot(q_ref[g, :, at], block)
            normed_ref[g, :, at] = head_norm(total, means, 1e-05)
    mixed = dot(normed_ref[...].reshape(groups * patches, width), close_ref[:width, :])
    out_ref[...] = (y_ref[...] + mixed.reshape(groups, patches, width)).astype(BF16)


def call(kernel, breadth, outs, args, scratch=(), flops=10**9, name=None):
    def place(a):
        return pl.BlockSpec(memory_space=SMEM if a.size <= 64 else VMEM)

    return pl.pallas_call(
        functools.partial(kernel, breadth),
        out_shape=[jax.ShapeDtypeStruct(s, d) for s, d in outs],
        in_specs=[place(a) for a in args],
        out_specs=[pl.BlockSpec(memory_space=VMEM) for _ in outs],
        scratch_shapes=[pltpu.VMEM(s, d) for s, d in scratch],
        compiler_params=pltpu.CompilerParams(vmem_limit_bytes=24 * 2**20),
        cost_estimate=pl.CostEstimate(flops=flops, bytes_accessed=2**20, transcendentals=0),
        name=name,
    )(*args)


def swap_with(value, axis, partner):
    size = lax.axis_size(axis)
    pairs = [(i, partner(i)) for i in range(size) if 0 <= partner(i) < size]
    return lax.ppermute(value, axis, pairs)


def entering(keep, give):
    core, chip = lax.axis_index("tm") % 2, lax.axis_index("tm") // 2
    chips = lax.axis_size("tm") // 2
    got = swap_with(give, "tm", lambda i: i ^ 1)
    total = (keep + got.astype(F32)).astype(BF16)
    before = jnp.zeros_like(keep)
    for m in range(1, chips):
        piece = swap_with(total, "tm", lambda i: i ^ (2 * m))
        before += jnp.where((chip ^ m) < chip, piece.astype(F32), 0.0)
    send = (before + jnp.where(core == 0, keep, 0.0)).astype(BF16)
    mine = before + jnp.where(core == 0, 0.0, got.astype(F32))
    other = swap_with(send, "tm", lambda i: i ^ 1)
    return mine, other


def per_device(x, w, close, sharp, table, tally):
    groups, patches, width = x.shape
    breadth = width // sharp.shape[0]
    x_odd = swap_with(x, "stations", lambda i: i + 2 * (i % 2) - 1)
    x_even = swap_with(x, "stations", lambda i: i ^ 1)
    block = x.shape
    part = (groups, breadth, HALF)
    normed, k, v, keep, give = call(
        states_kernel, breadth, [(block, BF16)] * 3 + [(part, F32), (part, BF16)], (x, w), name="states"
    )
    mine, other = entering(keep, give)
    q, lin, num, den = call(
        own_kernel, breadth, [(block, BF16)] + [(block, F32)] * 3, (normed, w, k, v, sharp, table, tally), name="own"
    )
    half = [((groups, patches, HALF), BF16)] * 2
    num, den = call(
        even_kernel, breadth, [(block, F32)] * 2, (x_even, w, q, sharp, table, tally, num, den), half, name="even"
    )
    (y,) = call(
        odd_kernel,
        breadth,
        [(block, F32)],
        (x_odd, w, q, sharp, table, tally, num, den, x, close),
        half + [(block, BF16)],
        name="odd",
    )
    (out,) = call(
        closing_kernel, breadth, [(block, BF16)], (q, lin, mine, other, close, y), [(block, BF16)], name="closing"
    )
    return out


def solution(mesh):
    return jax.shard_map(
        per_device,
        mesh=mesh,
        in_specs=(P("stations", "tm", None), P(), P(), P(), P("stations", None), P("stations")),
        out_specs=P("stations", "tm", None),
        check_vma=False,
    )
```

```python
import functools
import math

import jax
import jax.numpy as jnp
from jax import lax
from jax.experimental import pallas as pl
from jax.experimental.pallas import tpu as pltpu
from jax.sharding import PartitionSpec as P

NEAR = 4
HALF = 256
PAIR = 128
T = 32
F32 = jnp.float32
BF16 = jnp.bfloat16
VMEM = pltpu.VMEM
SMEM = pltpu.SMEM


def dot(a, b):
    return jnp.dot(a, b, preferred_element_type=F32)


def dot_nt(a, b):
    return lax.dot_general(a, b, (((1,), (1,)), ((), ())), preferred_element_type=F32)


def dot_tn(a, b):
    return lax.dot_general(a, b, (((0,), (0,)), ((), ())), preferred_element_type=F32)


def row_norm(x):
    xf = x.astype(F32)
    return (xf * lax.rsqrt(jnp.mean(xf * xf, axis=-1, keepdims=True) + 1e-06)).astype(BF16)


def head_ids(shape, axis, breadth):
    return lax.broadcasted_iota(jnp.int32, shape, axis) // breadth


def mean_matrix(breadth):
    same = head_ids((HALF, HALF), 0, breadth) == head_ids((HALF, HALF), 1, breadth)
    return jnp.where(same, 1.0 / breadth, 0.0).astype(BF16)


def head_norm(values, means, epsilon):
    square = (values * values).astype(BF16)
    return (values * lax.rsqrt(dot(square, means) + epsilon)).astype(BF16)


def own_head(values, j, breadth):
    ids = head_ids(values.shape, 1, breadth)
    return jnp.where(ids == j, values, jnp.zeros_like(values))


def multiplicity_mask(table_ref, tally_ref, base):
    groups, slots = table_ref.shape
    wide = groups * T
    ids = base + lax.broadcasted_iota(jnp.int32, (8, wide), 1) // T
    rows = []
    for g in range(groups):
        total = jnp.zeros((8, wide), F32)
        for j in range(slots):
            total += jnp.where((ids == table_ref[g, j]) & (j < tally_ref[g]), 1.0, 0.0)
        rows.append(jnp.broadcast_to(total[:1], (T, wide)))
    full = jnp.concatenate(rows, axis=0)
    t_row = lax.broadcasted_iota(jnp.int32, (wide, wide), 0) % T
    t_col = lax.broadcasted_iota(jnp.int32, (wide, wide), 1) % T
    return jnp.where(t_row == t_col, full, 0.0)


def pick(low, high, breadth):
    return jnp.where(head_ids(low.shape, 1, breadth) == 0, low, high)


def stack(values, breadth):
    return jnp.concatenate([own_head(values, j, breadth) for j in range(PAIR // breadth)], axis=0)


def cut(ref, c, u):
    groups = ref.shape[0]
    return ref[:, c * T : (c + 1) * T, u * PAIR : (u + 1) * PAIR].reshape(groups * T, PAIR)


def project(normed, w_ref, first, count):
    return [dot(normed, w_ref[:, first + h * HALF : first + (h + 1) * HALF]) for h in range(count)]


def keys_values(x_ref, w_ref, k_ref, v_ref, breadth):
    groups, patches, width = x_ref.shape
    halves = width // HALF
    means = mean_matrix(breadth)
    normed = row_norm(x_ref[...].reshape(groups * patches, width))
    keys = project(normed, w_ref, width, halves)
    values = project(normed, w_ref, 2 * width, halves)
    for h in range(halves):
        at = slice(h * HALF, (h + 1) * HALF)
        v_ref[:, :, at] = values[h].astype(BF16).reshape(groups, patches, HALF)
        k_ref[:, :, at] = head_norm(keys[h], means, 1e-06).reshape(groups, patches, HALF)
    return normed


def staggered(items, *stages):
    held = [{} for _ in stages]
    for i in range(len(items) + len(stages) - 1):
        for s, stage in enumerate(stages):
            if 0 <= i - s < len(items):
                before = (held[s - 1].pop(i - s),) if s else ()
                held[s][i - s] = stage(*before, *items[i - s])


def neighbours(breadth, q_ref, windows, sharp_ref, emit):
    groups, patches, width = q_ref.shape
    wide = groups * T
    heads = PAIR // breadth
    ones = stack(jnp.ones((wide, PAIR), BF16), breadth)
    scale = math.log2(math.e) / math.sqrt(breadth)
    lane = lax.broadcasted_iota(jnp.int32, (1, heads * wide), 1) // wide
    sharps = []
    for u in range(width // PAIR):
        row = jnp.full((1, heads * wide), sharp_ref[u * heads] * scale, F32)
        for j in range(1, heads):
            row = jnp.where(lane == j, sharp_ref[u * heads + j] * scale, row)
        sharps.append(row)
    masks = [jnp.concatenate([mask] * heads, axis=1) for _, _, mask in windows]
    sums = {}

    def score(u, c, n):
        return dot_nt(cut(q_ref, c, u), stack(cut(windows[n][0], c, u), breadth))

    def share(scores, u, c, n):
        return (jnp.exp2(scores * sharps[u]) * masks[n]).astype(BF16)

    def gather(shares, u, c, n):
        spread = jnp.concatenate([stack(cut(windows[n][1], c, u), breadth), ones], axis=1)
        part = dot(shares, spread)
        total = sums.pop((u, c)) + part if n else part
        if n + 1 < len(windows):
            sums[(u, c)] = total
        else:
            emit(c, u, total)

    items = [(u, c, n) for u in range(width // PAIR) for c in range(patches // T) for n in range(len(windows))]
    staggered(items, score, share, gather)


def states_kernel(breadth, x_ref, w_ref, n_ref, k_ref, v_ref, keep_ref, give_ref):
    groups, patches, width = x_ref.shape
    core = lax.axis_index("tm") % 2
    normed = keys_values(x_ref, w_ref, k_ref, v_ref, breadth)
    n_ref[...] = normed.reshape(n_ref.shape)
    for h in range(width // HALF):
        states = []
        for g in range(groups):
            pairs = []
            for u in range(h * HALF // PAIR, (h + 1) * HALF // PAIR):
                at = slice(u * PAIR, (u + 1) * PAIR)
                full = dot_tn(k_ref[g, :, at], v_ref[g, :, at])
                pairs.append(pick(full[:breadth], full[breadth:], breadth))
            states.append(jnp.concatenate(pairs, axis=1))

        @pl.when(core == h)
        def _():
            for g in range(groups):
                keep_ref[g] = states[g]

        @pl.when(core != h)
        def _():
            for g in range(groups):
                give_ref[g] = states[g].astype(BF16)


def own_kernel(breadth, n_ref, w_ref, k_ref, v_ref, q_ref, lin_ref):
    groups, patches, width = n_ref.shape
    halves = width // HALF
    means = mean_matrix(breadth)
    wide = (patches, patches * (PAIR // breadth))
    causal = lax.broadcasted_iota(jnp.int32, wide, 0) >= lax.broadcasted_iota(jnp.int32, wide, 1) % patches
    queries = project(n_ref[...].reshape(groups * patches, width), w_ref, 0, halves)
    for h in range(halves):
        q = head_norm(queries[h], means, 1e-06)
        q_ref[:, :, h * HALF : (h + 1) * HALF] = q.reshape(groups, patches, HALF)

    def score(h, g):
        scores = []
        for u in range(h * HALF // PAIR, (h + 1) * HALF // PAIR):
            at = slice(u * PAIR, (u + 1) * PAIR)
            scores.append(dot_nt(q_ref[g, :, at], stack(k_ref[g, :, at], breadth)))
        return scores

    def share(scores, h, g):
        return jnp.concatenate([jnp.where(causal, s, 0.0).astype(BF16) for s in scores], axis=1)

    def gather(shares, h, g):
        at = slice(h * HALF, (h + 1) * HALF)
        v = v_ref[g, :, at]
        spread = jnp.concatenate([own_head(v, j, breadth) for j in range(HALF // breadth)], axis=0)
        lin_ref[g, :, at] = dot(shares, spread)

    staggered([(h, g) for h in range(halves) for g in range(groups)], score, share, gather)


def even_kernel(breadth, x_ref, w_ref, k_ref, v_ref, q_ref, sharp_ref, table_ref, tally_ref, keep_ref, acc_ref, kept_ref, ke_ref, ve_ref):
    groups, patches, width = x_ref.shape
    station = lax.axis_index("stations")
    keys_values(x_ref, w_ref, ke_ref, ve_ref, breadth)
    windows = [
        (k_ref, v_ref, multiplicity_mask(table_ref, tally_ref, station * groups)),
        (ke_ref, ve_ref, multiplicity_mask(table_ref, tally_ref, (station ^ 1) * groups)),
    ]

    def emit(c, u, total):
        acc_ref[:, c * T : (c + 1) * T, u * 2 * PAIR : (u + 1) * 2 * PAIR] = total.reshape(groups, T, 2 * PAIR)

    neighbours(breadth, q_ref, windows, sharp_ref, emit)


def odd_kernel(breadth, x_ref, w_ref, q_ref, sharp_ref, table_ref, tally_ref, acc_ref, own_ref, close_ref, y_ref, k_ref, v_ref, gathered_ref):
    groups, patches, width = x_ref.shape
    station = lax.axis_index("stations")
    base = (station + 2 * (station % 2) - 1) * groups
    keys_values(x_ref, w_ref, k_ref, v_ref, breadth)
    windows = [(k_ref, v_ref, multiplicity_mask(table_ref, tally_ref, base))]

    def emit(c, u, total):
        span = slice(c * T, (c + 1) * T)
        total = total.reshape(groups, T, 2 * PAIR) + acc_ref[:, span, u * 2 * PAIR : (u + 1) * 2 * PAIR]
        gathered_ref[:, span, u * PAIR : (u + 1) * PAIR] = (total[:, :, :PAIR] / total[:, :, PAIR:]).astype(BF16)

    neighbours(breadth, q_ref, windows, sharp_ref, emit)
    mixed = dot(gathered_ref[...].reshape(groups * patches, width), close_ref[width:, :])
    y_ref[...] = own_ref[...].astype(F32) + mixed.reshape(groups, patches, width)


def closing_kernel(breadth, q_ref, lin_ref, mine_ref, other_ref, close_ref, y_ref, out_ref, normed_ref):
    groups, patches, width = q_ref.shape
    heads = HALF // breadth
    halves = width // HALF
    core = lax.axis_index("tm") % 2
    means = mean_matrix(breadth)
    same = head_ids((HALF, HALF), 0, breadth) == head_ids((HALF, HALF), 1, breadth)
    totals = []
    for h in range(halves):
        at = slice(h * HALF, (h + 1) * HALF)
        for g in range(groups):
            state = jnp.where(core == h, mine_ref[g], other_ref[g].astype(F32)).astype(BF16)
            block = jnp.where(same, jnp.concatenate([state] * heads, axis=0), jnp.zeros((), BF16))
            totals.append(lin_ref[g, :, at] + dot(q_ref[g, :, at], block))
    for h in range(halves):
        total = jnp.concatenate(totals[h * groups : (h + 1) * groups], axis=0)
        normed_ref[:, h * HALF : (h + 1) * HALF] = head_norm(total, means, 1e-05)
    mixed = dot(normed_ref[...], close_ref[:width, :])
    out_ref[...] = (y_ref[...] + mixed.reshape(groups, patches, width)).astype(BF16)


def call(kernel, breadth, outs, args, scratch=(), flops=10**9, name=None, through=None):
    def place(a):
        return pl.BlockSpec(memory_space=SMEM if a.size <= 64 else VMEM)

    in_specs, out_specs = [place(a) for a in args], [pl.BlockSpec(memory_space=VMEM) for _ in outs]
    aliases = {}
    if through is not None:
        in_specs[through[0]] = out_specs[through[1]] = pl.BlockSpec(memory_space=pl.ANY)
        aliases = {through[0]: through[1]}
    return pl.pallas_call(
        functools.partial(kernel, breadth),
        out_shape=[jax.ShapeDtypeStruct(s, d) for s, d in outs],
        in_specs=in_specs,
        out_specs=out_specs,
        scratch_shapes=[pltpu.VMEM(s, d) for s, d in scratch],
        input_output_aliases=aliases,
        compiler_params=pltpu.CompilerParams(vmem_limit_bytes=10 * 2**20),
        cost_estimate=pl.CostEstimate(flops=flops, bytes_accessed=2**20, transcendentals=0),
        name=name,
    )(*args)


def swap_with(value, axis, partner):
    size = lax.axis_size(axis)
    pairs = [(i, partner(i)) for i in range(size) if 0 <= partner(i) < size]
    return lax.ppermute(value, axis, pairs)


def per_device(x, w, close, sharp, table, tally):
    groups, patches, width = x.shape
    breadth = width // sharp.shape[0]
    core, chip = lax.axis_index("tm") % 2, lax.axis_index("tm") // 2
    chips = lax.axis_size("tm") // 2
    block = x.shape
    part = (groups, breadth, HALF)
    x_odd = swap_with(x, "stations", lambda i: i + 2 * (i % 2) - 1)
    x_even = swap_with(x, "stations", lambda i: i ^ 1)
    normed, k, v, keep, give = call(
        states_kernel, breadth, [(block, BF16)] * 3 + [(part, F32), (part, BF16)], (x, w), name="states"
    )
    got = swap_with(give, "tm", lambda i: i ^ 1)
    total = (keep + got.astype(F32)).astype(BF16)
    pieces = [swap_with(total, "tm", lambda i: i ^ (2 * m)) for m in range(1, chips)]
    q, lin = call(own_kernel, breadth, [(block, BF16), (block, F32)], (normed, w, k, v), name="own")
    acc, keep = call(
        even_kernel,
        breadth,
        [((groups, patches, 2 * width), F32), (part, F32)],
        (x_even, w, k, v, q, sharp, table, tally, keep),
        [(block, BF16)] * 2,
        name="even",
        through=(8, 1),
    )
    before = jnp.zeros_like(keep)
    for m, piece in enumerate(pieces, 1):
        before += jnp.where((chip ^ m) < chip, piece.astype(F32), 0.0)
    send = (before + jnp.where(core == 0, keep, 0.0)).astype(BF16)
    mine = before + jnp.where(core == 0, 0.0, got.astype(F32))
    other = swap_with(send, "tm", lambda i: i ^ 1)
    (y,) = call(
        odd_kernel,
        breadth,
        [(block, F32)],
        (x_odd, w, q, sharp, table, tally, acc, x, close),
        [(block, BF16)] * 3,
        name="odd",
    )
    (out,) = call(
        closing_kernel,
        breadth,
        [(block, BF16)],
        (q, lin, mine, other, close, y),
        [((groups * patches, width), BF16)],
        name="closing",
    )
    return out


def solution(mesh):
    return jax.shard_map(
        per_device,
        mesh=mesh,
        in_specs=(P("stations", "tm", None), P(), P(), P(), P("stations", None), P("stations")),
        out_specs=P("stations", "tm", None),
        check_vma=False,
    )
```

```python
import functools
import math

import jax
import jax.numpy as jnp
from jax import lax
from jax.experimental import pallas as pl
from jax.experimental.pallas import tpu as pltpu
from jax.sharding import PartitionSpec as P

NEAR = 4
HALF = 256
PAIR = 128
T = 32
F32 = jnp.float32
BF16 = jnp.bfloat16
VMEM = pltpu.VMEM
SMEM = pltpu.SMEM


def dot(a, b):
    return jnp.dot(a, b, preferred_element_type=F32)


def dot_nt(a, b):
    return lax.dot_general(a, b, (((1,), (1,)), ((), ())), preferred_element_type=F32)


def dot_tn(a, b):
    return lax.dot_general(a, b, (((0,), (0,)), ((), ())), preferred_element_type=F32)


def row_norm(x):
    xf = x.astype(F32)
    return (xf * lax.rsqrt(jnp.mean(xf * xf, axis=-1, keepdims=True) + 1e-06)).astype(BF16)


def head_ids(shape, axis, breadth):
    return lax.broadcasted_iota(jnp.int32, shape, axis) // breadth


def mean_matrix(breadth):
    same = head_ids((HALF, HALF), 0, breadth) == head_ids((HALF, HALF), 1, breadth)
    return jnp.where(same, 1.0 / breadth, 0.0).astype(BF16)


def head_norm(values, means, epsilon):
    square = (values * values).astype(BF16)
    return (values * lax.rsqrt(dot(square, means) + epsilon)).astype(BF16)


def own_head(values, j, breadth):
    ids = head_ids(values.shape, 1, breadth)
    return jnp.where(ids == j, values, jnp.zeros_like(values))


def multiplicity_mask(table_ref, tally_ref, base):
    groups, slots = table_ref.shape
    wide = groups * T
    ids = base + lax.broadcasted_iota(jnp.int32, (8, wide), 1) // T
    rows = []
    for g in range(groups):
        total = jnp.zeros((8, wide), F32)
        for j in range(slots):
            total += jnp.where((ids == table_ref[g, j]) & (j < tally_ref[g]), 1.0, 0.0)
        rows.append(jnp.broadcast_to(total[:1], (T, wide)))
    full = jnp.concatenate(rows, axis=0)
    t_row = lax.broadcasted_iota(jnp.int32, (wide, wide), 0) % T
    t_col = lax.broadcasted_iota(jnp.int32, (wide, wide), 1) % T
    return jnp.where(t_row == t_col, full, 0.0)


def pick(low, high, breadth):
    return jnp.where(head_ids(low.shape, 1, breadth) == 0, low, high)


def stack(values, breadth):
    return jnp.concatenate([own_head(values, j, breadth) for j in range(PAIR // breadth)], axis=0)


def cut(ref, c, u):
    groups = ref.shape[0]
    return ref[:, c * T : (c + 1) * T, u * PAIR : (u + 1) * PAIR].reshape(groups * T, PAIR)


def project(normed, w_ref, first, count):
    return [dot(normed, w_ref[:, first + h * HALF : first + (h + 1) * HALF]) for h in range(count)]


def keys_values(x_ref, w_ref, k_ref, v_ref, breadth):
    groups, patches, width = x_ref.shape
    halves = width // HALF
    means = mean_matrix(breadth)
    normed = row_norm(x_ref[...].reshape(groups * patches, width))
    keys = project(normed, w_ref, width, halves)
    values = project(normed, w_ref, 2 * width, halves)
    for h in range(halves):
        at = slice(h * HALF, (h + 1) * HALF)
        v_ref[:, :, at] = values[h].astype(BF16).reshape(groups, patches, HALF)
        k_ref[:, :, at] = head_norm(keys[h], means, 1e-06).reshape(groups, patches, HALF)


def staggered(items, *stages):
    held = [{} for _ in stages]
    for i in range(len(items) + len(stages) - 1):
        for s, stage in enumerate(stages):
            if 0 <= i - s < len(items):
                before = (held[s - 1].pop(i - s),) if s else ()
                held[s][i - s] = stage(*before, *items[i - s])


def neighbours(breadth, q_ref, windows, sharp_ref, emit):
    groups, patches, width = q_ref.shape
    wide = groups * T
    heads = PAIR // breadth
    ones = stack(jnp.ones((wide, PAIR), BF16), breadth)
    scale = math.log2(math.e) / math.sqrt(breadth)
    lane = lax.broadcasted_iota(jnp.int32, (1, heads * wide), 1) // wide
    sharps = []
    for u in range(width // PAIR):
        row = jnp.full((1, heads * wide), sharp_ref[u * heads] * scale, F32)
        for j in range(1, heads):
            row = jnp.where(lane == j, sharp_ref[u * heads + j] * scale, row)
        sharps.append(row)
    sums = {}

    def score(u, c, n):
        return dot_nt(cut(q_ref, c, u), stack(cut(windows[n][0], c, u), breadth))

    def share(scores, u, c, n):
        return (jnp.exp2(scores * sharps[u]) * windows[n][2][...]).astype(BF16)

    def gather(shares, u, c, n):
        spread = jnp.concatenate([stack(cut(windows[n][1], c, u), breadth), ones], axis=1)
        part = dot(shares, spread)
        total = sums.pop((u, c)) + part if n else part
        if n + 1 < len(windows):
            sums[(u, c)] = total
        else:
            emit(c, u, total)

    items = [(u, c, n) for u in range(width // PAIR) for c in range(patches // T) for n in range(len(windows))]
    staggered(items, score, share, gather)


def masks_kernel(breadth, table_ref, tally_ref, mask_ref):
    groups = table_ref.shape[0]
    station = lax.axis_index("stations")
    around = (station, station ^ 1, station + 2 * (station % 2) - 1)
    for n, place in enumerate(around):
        mask = multiplicity_mask(table_ref, tally_ref, place * groups)
        mask_ref[n] = jnp.concatenate([mask] * (PAIR // breadth), axis=1)


def states_kernel(breadth, x_ref, w_ref, mask_ref, k_ref, v_ref, keep_ref, give_ref):
    groups, patches, width = x_ref.shape
    core = lax.axis_index("tm") % 2
    keys_values(x_ref, w_ref, k_ref, v_ref, breadth)
    for h in range(width // HALF):
        states = []
        for g in range(groups):
            pairs = []
            for u in range(h * HALF // PAIR, (h + 1) * HALF // PAIR):
                at = slice(u * PAIR, (u + 1) * PAIR)
                full = dot_tn(k_ref[g, :, at], v_ref[g, :, at])
                pairs.append(pick(full[:breadth], full[breadth:], breadth))
            states.append(jnp.concatenate(pairs, axis=1))

        @pl.when(core == h)
        def _():
            for g in range(groups):
                keep_ref[g] = states[g]

        @pl.when(core != h)
        def _():
            for g in range(groups):
                give_ref[g] = states[g].astype(BF16)


def own_kernel(breadth, x_ref, w_ref, k_ref, v_ref, q_ref, lin_ref):
    groups, patches, width = x_ref.shape
    halves = width // HALF
    means = mean_matrix(breadth)
    wide = (patches, patches * (PAIR // breadth))
    causal = lax.broadcasted_iota(jnp.int32, wide, 0) >= lax.broadcasted_iota(jnp.int32, wide, 1) % patches
    queries = project(row_norm(x_ref[...].reshape(groups * patches, width)), w_ref, 0, halves)
    for h in range(halves):
        q = head_norm(queries[h], means, 1e-06)
        q_ref[:, :, h * HALF : (h + 1) * HALF] = q.reshape(groups, patches, HALF)

    def score(h, g):
        scores = []
        for u in range(h * HALF // PAIR, (h + 1) * HALF // PAIR):
            at = slice(u * PAIR, (u + 1) * PAIR)
            scores.append(dot_nt(q_ref[g, :, at], stack(k_ref[g, :, at], breadth)))
        return scores

    def share(scores, h, g):
        return jnp.concatenate([jnp.where(causal, s, 0.0).astype(BF16) for s in scores], axis=1)

    def gather(shares, h, g):
        at = slice(h * HALF, (h + 1) * HALF)
        v = v_ref[g, :, at]
        spread = jnp.concatenate([own_head(v, j, breadth) for j in range(HALF // breadth)], axis=0)
        lin_ref[g, :, at] = dot(shares, spread)

    staggered([(h, g) for h in range(halves) for g in range(groups)], score, share, gather)


def even_kernel(breadth, x_ref, w_ref, k_ref, v_ref, q_ref, sharp_ref, mask_ref, keep_ref, acc_ref, kept_ref, ke_ref, ve_ref):
    groups, patches, width = x_ref.shape
    keys_values(x_ref, w_ref, ke_ref, ve_ref, breadth)
    windows = [
        (k_ref, v_ref, mask_ref.at[0]),
        (ke_ref, ve_ref, mask_ref.at[1]),
    ]

    def emit(c, u, total):
        acc_ref[:, c * T : (c + 1) * T, u * 2 * PAIR : (u + 1) * 2 * PAIR] = total.reshape(groups, T, 2 * PAIR)

    neighbours(breadth, q_ref, windows, sharp_ref, emit)


def odd_kernel(breadth, x_ref, w_ref, q_ref, sharp_ref, mask_ref, acc_ref, own_ref, close_ref, y_ref, k_ref, v_ref, gathered_ref):
    groups, patches, width = x_ref.shape
    keys_values(x_ref, w_ref, k_ref, v_ref, breadth)
    windows = [(k_ref, v_ref, mask_ref.at[2])]

    def emit(c, u, total):
        span = slice(c * T, (c + 1) * T)
        total = total.reshape(groups, T, 2 * PAIR) + acc_ref[:, span, u * 2 * PAIR : (u + 1) * 2 * PAIR]
        gathered_ref[:, span, u * PAIR : (u + 1) * PAIR] = (total[:, :, :PAIR] / total[:, :, PAIR:]).astype(BF16)

    neighbours(breadth, q_ref, windows, sharp_ref, emit)
    mixed = dot(gathered_ref[...].reshape(groups * patches, width), close_ref[width:, :])
    y_ref[...] = own_ref[...].astype(F32) + mixed.reshape(groups, patches, width)


def closing_kernel(breadth, q_ref, lin_ref, mine_ref, other_ref, close_ref, y_ref, out_ref, normed_ref):
    groups, patches, width = q_ref.shape
    heads = HALF // breadth
    halves = width // HALF
    core = lax.axis_index("tm") % 2
    means = mean_matrix(breadth)
    same = head_ids((HALF, HALF), 0, breadth) == head_ids((HALF, HALF), 1, breadth)
    totals = []
    for h in range(halves):
        at = slice(h * HALF, (h + 1) * HALF)
        for g in range(groups):
            state = jnp.where(core == h, mine_ref[g], other_ref[g])
            block = jnp.where(same, jnp.concatenate([state] * heads, axis=0), jnp.zeros((), BF16))
            totals.append(lin_ref[g, :, at] + dot(q_ref[g, :, at], block))
    for h in range(halves):
        total = jnp.concatenate(totals[h * groups : (h + 1) * groups], axis=0)
        normed_ref[:, h * HALF : (h + 1) * HALF] = head_norm(total, means, 1e-05)
    mixed = dot(normed_ref[...], close_ref[:width, :])
    out_ref[...] = (y_ref[...] + mixed.reshape(groups, patches, width)).astype(BF16)


def combine_kernel(breadth, keep_ref, got_ref, total_ref):
    total_ref[...] = (keep_ref[...] + got_ref[...].astype(F32)).astype(BF16)


def carry_kernel(breadth, keep_ref, got_ref, *refs):
    *pieces, send_ref, mine_ref = refs
    core, chip = lax.axis_index("tm") % 2, lax.axis_index("tm") // 2
    before = jnp.zeros(keep_ref.shape, F32)
    for m, piece in enumerate(pieces, 1):
        before += jnp.where((chip ^ m) < chip, piece[...].astype(F32), 0.0)
    send_ref[...] = (before + jnp.where(core == 0, keep_ref[...], 0.0)).astype(BF16)
    mine_ref[...] = (before + jnp.where(core == 0, 0.0, got_ref[...].astype(F32))).astype(BF16)


def call(kernel, breadth, outs, args, scratch=(), flops=3 * 10**9, name=None, through=None):
    def place(a):
        return pl.BlockSpec(memory_space=SMEM if a.size <= 64 else VMEM)

    in_specs, out_specs = [place(a) for a in args], [pl.BlockSpec(memory_space=VMEM) for _ in outs]
    for i, o in (through or {}).items():
        in_specs[i] = pl.BlockSpec(memory_space=pl.ANY)
        if o is not None:
            out_specs[o] = in_specs[i]
    return pl.pallas_call(
        functools.partial(kernel, breadth),
        out_shape=[jax.ShapeDtypeStruct(s, d) for s, d in outs],
        in_specs=in_specs,
        out_specs=out_specs,
        scratch_shapes=[pltpu.VMEM(s, d) for s, d in scratch],
        input_output_aliases={i: o for i, o in (through or {}).items() if o is not None},
        compiler_params=pltpu.CompilerParams(vmem_limit_bytes=10 * 2**20),
        cost_estimate=pl.CostEstimate(flops=flops, bytes_accessed=2**20, transcendentals=0),
        name=name,
    )(*args)


def swap_with(value, axis, partner):
    size = lax.axis_size(axis)
    pairs = [(i, partner(i)) for i in range(size) if 0 <= partner(i) < size]
    return lax.ppermute(value, axis, pairs)


def per_device(x, w, close, sharp, table, tally):
    groups, patches, width = x.shape
    breadth = width // sharp.shape[0]
    chips = lax.axis_size("tm") // 2
    block = x.shape
    part = (groups, breadth, HALF)
    x_odd = swap_with(x, "stations", lambda i: i + 2 * (i % 2) - 1)
    x_even = swap_with(x, "stations", lambda i: i ^ 1)
    wide = groups * T
    (masks,) = call(masks_kernel, breadth, [((3, wide, wide * PAIR // breadth), F32)], (table, tally), name="masks")
    k, v, keep, give = call(
        states_kernel,
        breadth,
        [(block, BF16)] * 2 + [(part, F32), (part, BF16)],
        (x, w, masks),
        name="states",
        through={2: None},
    )
    got = swap_with(give, "tm", lambda i: i ^ 1)
    (total,) = call(combine_kernel, breadth, [(part, BF16)], (keep, got), name="combine")
    pieces = [swap_with(total, "tm", lambda i: i ^ (2 * m)) for m in range(1, chips)]
    q, lin = call(own_kernel, breadth, [(block, BF16), (block, F32)], (x, w, k, v), name="own")
    acc, keep = call(
        even_kernel,
        breadth,
        [((groups, patches, 2 * width), F32), (part, F32)],
        (x_even, w, k, v, q, sharp, masks, keep),
        [(block, BF16)] * 2,
        name="even",
        through={7: 1},
    )
    send, mine = call(carry_kernel, breadth, [(part, BF16)] * 2, (keep, got, *pieces), name="carry")
    other = swap_with(send, "tm", lambda i: i ^ 1)
    (y,) = call(
        odd_kernel,
        breadth,
        [(block, F32)],
        (x_odd, w, q, sharp, masks, acc, x, close),
        [(block, BF16)] * 3,
        name="odd",
    )
    (out,) = call(
        closing_kernel,
        breadth,
        [(block, BF16)],
        (q, lin, mine, other, close, y),
        [((groups * patches, width), BF16)],
        name="closing",
    )
    return out


def solution(mesh):
    return jax.shard_map(
        per_device,
        mesh=mesh,
        in_specs=(P("stations", "tm", None), P(), P(), P(), P("stations", None), P("stations")),
        out_specs=P("stations", "tm", None),
        check_vma=False,
    )
```

```python
import functools
import math

import jax
import jax.numpy as jnp
from jax import lax
from jax.experimental import pallas as pl
from jax.experimental.pallas import tpu as pltpu
from jax.sharding import PartitionSpec as P

NEAR = 4
HALF = 256
PAIR = 128
T = 32
F32 = jnp.float32
BF16 = jnp.bfloat16
VMEM = pltpu.VMEM
SMEM = pltpu.SMEM


def dot(a, b):
    return jnp.dot(a, b, preferred_element_type=F32)


def dot_nt(a, b):
    return lax.dot_general(a, b, (((1,), (1,)), ((), ())), preferred_element_type=F32)


def dot_tn(a, b):
    return lax.dot_general(a, b, (((0,), (0,)), ((), ())), preferred_element_type=F32)


def row_norm(x):
    xf = x.astype(F32)
    return (xf * lax.rsqrt(jnp.mean(xf * xf, axis=-1, keepdims=True) + 1e-06)).astype(BF16)


def head_ids(shape, axis, breadth):
    return lax.broadcasted_iota(jnp.int32, shape, axis) // breadth


def means_kernel(breadth, means_ref):
    same = head_ids((HALF, HALF), 0, breadth) == head_ids((HALF, HALF), 1, breadth)
    means_ref[...] = jnp.where(same, 1.0 / breadth, 0.0).astype(BF16)


def head_norm(values, means, epsilon):
    square = (values * values).astype(BF16)
    return (values * lax.rsqrt(dot(square, means) + epsilon)).astype(BF16)


def own_head(values, j, breadth):
    ids = head_ids(values.shape, 1, breadth)
    return jnp.where(ids == j, values, jnp.zeros_like(values))


def multiplicity_mask(table_ref, tally_ref, base):
    groups, slots = table_ref.shape
    wide = groups * T
    ids = base + lax.broadcasted_iota(jnp.int32, (8, wide), 1) // T
    rows = []
    for g in range(groups):
        total = jnp.zeros((8, wide), F32)
        for j in range(slots):
            total += jnp.where((ids == table_ref[g, j]) & (j < tally_ref[g]), 1.0, 0.0)
        rows.append(jnp.broadcast_to(total[:1], (T, wide)))
    full = jnp.concatenate(rows, axis=0)
    t_row = lax.broadcasted_iota(jnp.int32, (wide, wide), 0) % T
    t_col = lax.broadcasted_iota(jnp.int32, (wide, wide), 1) % T
    return jnp.where(t_row == t_col, full, 0.0)


def pick(low, high, breadth):
    return jnp.where(head_ids(low.shape, 1, breadth) == 0, low, high)


def stack(values, breadth):
    return jnp.concatenate([own_head(values, j, breadth) for j in range(PAIR // breadth)], axis=0)


def cut(ref, c, u):
    groups = ref.shape[0]
    return ref[:, c * T : (c + 1) * T, u * PAIR : (u + 1) * PAIR].reshape(groups * T, PAIR)


def project(normed, w_ref, first, count):
    return [dot(normed, w_ref[:, first + h * HALF : first + (h + 1) * HALF]) for h in range(count)]


def keys_values(x_ref, w_ref, means_ref, k_ref, v_ref, breadth):
    groups, patches, width = x_ref.shape
    halves = width // HALF
    means = means_ref[...]
    normed = row_norm(x_ref[...].reshape(groups * patches, width))
    keys = project(normed, w_ref, width, halves)
    values = project(normed, w_ref, 2 * width, halves)
    for h in range(halves):
        at = slice(h * HALF, (h + 1) * HALF)
        v_ref[:, :, at] = values[h].astype(BF16).reshape(groups, patches, HALF)
        k_ref[:, :, at] = head_norm(keys[h], means, 1e-06).reshape(groups, patches, HALF)


def staggered(items, *stages):
    held = [{} for _ in stages]
    for i in range(len(items) + len(stages) - 1):
        for s, stage in enumerate(stages):
            if 0 <= i - s < len(items):
                before = (held[s - 1].pop(i - s),) if s else ()
                held[s][i - s] = stage(*before, *items[i - s])


def neighbours(breadth, q_ref, windows, sharp_ref, emit):
    groups, patches, width = q_ref.shape
    wide = groups * T
    heads = PAIR // breadth
    ones = stack(jnp.ones((wide, PAIR), BF16), breadth)
    scale = math.log2(math.e) / math.sqrt(breadth)
    lane = lax.broadcasted_iota(jnp.int32, (1, heads * wide), 1) // wide
    sharps = []
    for u in range(width // PAIR):
        row = jnp.full((1, heads * wide), sharp_ref[u * heads] * scale, F32)
        for j in range(1, heads):
            row = jnp.where(lane == j, sharp_ref[u * heads + j] * scale, row)
        sharps.append(row)
    sums = {}

    def score(u, c, n):
        return dot_nt(cut(q_ref, c, u), stack(cut(windows[n][0], c, u), breadth))

    def share(scores, u, c, n):
        return (jnp.exp2(scores * sharps[u]) * windows[n][2][...]).astype(BF16)

    def gather(shares, u, c, n):
        spread = jnp.concatenate([stack(cut(windows[n][1], c, u), breadth), ones], axis=1)
        part = dot(shares, spread)
        total = sums.pop((u, c)) + part if n else part
        if n + 1 < len(windows):
            sums[(u, c)] = total
        else:
            emit(c, u, total)

    items = [(u, c, n) for u in range(width // PAIR) for c in range(patches // T) for n in range(len(windows))]
    staggered(items, score, share, gather)


def masks_kernel(breadth, table_ref, tally_ref, total_ref, mask_ref):
    groups = table_ref.shape[0]
    station = lax.axis_index("stations")
    around = (station, station ^ 1, station + 2 * (station % 2) - 1)
    for n, place in enumerate(around):
        mask = multiplicity_mask(table_ref, tally_ref, place * groups)
        mask_ref[n] = jnp.concatenate([mask] * (PAIR // breadth), axis=1)


def states_kernel(breadth, x_ref, w_ref, means_ref, k_ref, v_ref, keep_ref, give_ref):
    groups, patches, width = x_ref.shape
    core = lax.axis_index("tm") % 2
    keys_values(x_ref, w_ref, means_ref, k_ref, v_ref, breadth)
    for h in range(width // HALF):
        states = []
        for g in range(groups):
            pairs = []
            for u in range(h * HALF // PAIR, (h + 1) * HALF // PAIR):
                at = slice(u * PAIR, (u + 1) * PAIR)
                full = dot_tn(k_ref[g, :, at], v_ref[g, :, at])
                pairs.append(pick(full[:breadth], full[breadth:], breadth))
            states.append(jnp.concatenate(pairs, axis=1))

        @pl.when(core == h)
        def _():
            for g in range(groups):
                keep_ref[g] = states[g]

        @pl.when(core != h)
        def _():
            for g in range(groups):
                give_ref[g] = states[g].astype(BF16)


def own_kernel(breadth, x_ref, w_ref, means_ref, k_ref, v_ref, total_ref, q_ref, lin_ref):
    groups, patches, width = x_ref.shape
    halves = width // HALF
    means = means_ref[...]
    wide = (patches, patches * (PAIR // breadth))
    causal = lax.broadcasted_iota(jnp.int32, wide, 0) >= lax.broadcasted_iota(jnp.int32, wide, 1) % patches
    queries = project(row_norm(x_ref[...].reshape(groups * patches, width)), w_ref, 0, halves)
    for h in range(halves):
        q = head_norm(queries[h], means, 1e-06)
        q_ref[:, :, h * HALF : (h + 1) * HALF] = q.reshape(groups, patches, HALF)

    def score(h, g):
        scores = []
        for u in range(h * HALF // PAIR, (h + 1) * HALF // PAIR):
            at = slice(u * PAIR, (u + 1) * PAIR)
            scores.append(dot_nt(q_ref[g, :, at], stack(k_ref[g, :, at], breadth)))
        return scores

    def share(scores, h, g):
        return jnp.concatenate([jnp.where(causal, s, 0.0).astype(BF16) for s in scores], axis=1)

    def gather(shares, h, g):
        at = slice(h * HALF, (h + 1) * HALF)
        v = v_ref[g, :, at]
        spread = jnp.concatenate([own_head(v, j, breadth) for j in range(HALF // breadth)], axis=0)
        lin_ref[g, :, at] = dot(shares, spread)

    staggered([(h, g) for h in range(halves) for g in range(groups)], score, share, gather)


def near_kernel(breadth, k_ref, v_ref, q_ref, sharp_ref, mask_ref, acc_ref):
    groups = q_ref.shape[0]

    def emit(c, u, total):
        acc_ref[:, c * T : (c + 1) * T, u * 2 * PAIR : (u + 1) * 2 * PAIR] = total.reshape(groups, T, 2 * PAIR)

    neighbours(breadth, q_ref, [(k_ref, v_ref, mask_ref.at[0])], sharp_ref, emit)


def even_kernel(breadth, x_ref, w_ref, means_ref, q_ref, sharp_ref, mask_ref, acc_ref, keep_ref, sum_ref, kept_ref, k_ref, v_ref):
    groups = x_ref.shape[0]
    keys_values(x_ref, w_ref, means_ref, k_ref, v_ref, breadth)

    def emit(c, u, total):
        at = (slice(None), slice(c * T, (c + 1) * T), slice(u * 2 * PAIR, (u + 1) * 2 * PAIR))
        sum_ref[at] = acc_ref[at] + total.reshape(groups, T, 2 * PAIR)

    neighbours(breadth, q_ref, [(k_ref, v_ref, mask_ref.at[1])], sharp_ref, emit)


def closing_kernel(breadth, q_ref, lin_ref, mine_ref, other_ref, means_ref, close_ref, x_ref, y_ref, normed_ref):
    groups, patches, width = q_ref.shape
    heads = HALF // breadth
    halves = width // HALF
    core = lax.axis_index("tm") % 2
    means = means_ref[...]
    totals = []
    for h in range(halves):
        at = slice(h * HALF, (h + 1) * HALF)
        for g in range(groups):
            state = jnp.where(core == h, mine_ref[g], other_ref[g])
            block = jnp.where(means > 0, jnp.concatenate([state] * heads, axis=0), jnp.zeros((), BF16))
            totals.append(lin_ref[g, :, at] + dot(q_ref[g, :, at], block))
    for h in range(halves):
        total = jnp.concatenate(totals[h * groups : (h + 1) * groups], axis=0)
        normed_ref[:, h * HALF : (h + 1) * HALF] = head_norm(total, means, 1e-05)
    mixed = dot(normed_ref[...], close_ref[:width, :])
    y_ref[...] = x_ref[...].astype(F32) + mixed.reshape(groups, patches, width)


def odd_kernel(breadth, x_ref, w_ref, means_ref, q_ref, sharp_ref, mask_ref, acc_ref, close_ref, y_ref, out_ref, k_ref, v_ref, gathered_ref):
    groups, patches, width = x_ref.shape
    station = lax.axis_index("stations")
    partner = station + 2 * (station % 2) - 1
    there = (partner >= 0) & (partner < lax.axis_size("stations"))

    def part(c, u):
        return (slice(None), slice(c * T, (c + 1) * T), slice(u * 2 * PAIR, (u + 1) * 2 * PAIR))

    def finish(c, u, total):
        share = total[:, :, :PAIR] / total[:, :, PAIR:]
        gathered_ref[:, c * T : (c + 1) * T, u * PAIR : (u + 1) * PAIR] = share.astype(BF16)

    @pl.when(there)
    def _():
        keys_values(x_ref, w_ref, means_ref, k_ref, v_ref, breadth)

        def emit(c, u, total):
            finish(c, u, acc_ref[part(c, u)] + total.reshape(groups, T, 2 * PAIR))

        neighbours(breadth, q_ref, [(k_ref, v_ref, mask_ref.at[2])], sharp_ref, emit)

    @pl.when(jnp.logical_not(there))
    def _():
        for u in range(width // PAIR):
            for c in range(patches // T):
                finish(c, u, acc_ref[part(c, u)])

    mixed = dot(gathered_ref[...].reshape(groups * patches, width), close_ref[width:, :])
    out_ref[...] = (y_ref[...] + mixed.reshape(groups, patches, width)).astype(BF16)


def combine_kernel(breadth, keep_ref, got_ref, total_ref):
    total_ref[...] = (keep_ref[...] + got_ref[...].astype(F32)).astype(BF16)


def carry_kernel(breadth, keep_ref, got_ref, *refs):
    *pieces, send_ref, mine_ref = refs
    core, chip = lax.axis_index("tm") % 2, lax.axis_index("tm") // 2
    before = jnp.zeros(keep_ref.shape, F32)
    for m, piece in enumerate(pieces, 1):
        before += jnp.where((chip ^ m) < chip, piece[...].astype(F32), 0.0)
    send_ref[...] = (before + jnp.where(core == 0, keep_ref[...], 0.0)).astype(BF16)
    mine_ref[...] = (before + jnp.where(core == 0, 0.0, got_ref[...].astype(F32))).astype(BF16)


def call(kernel, breadth, outs, args, scratch=(), flops=10**9, name=None, through=None):
    def place(a):
        return pl.BlockSpec(memory_space=SMEM if a.size <= 64 else VMEM)

    in_specs, out_specs = [place(a) for a in args], [pl.BlockSpec(memory_space=VMEM) for _ in outs]
    for i, o in (through or {}).items():
        in_specs[i] = pl.BlockSpec(memory_space=pl.ANY)
        if o is not None:
            out_specs[o] = in_specs[i]
    return pl.pallas_call(
        functools.partial(kernel, breadth),
        out_shape=[jax.ShapeDtypeStruct(s, d) for s, d in outs],
        in_specs=in_specs,
        out_specs=out_specs,
        scratch_shapes=[pltpu.VMEM(s, d) for s, d in scratch],
        input_output_aliases={i: o for i, o in (through or {}).items() if o is not None},
        compiler_params=pltpu.CompilerParams(vmem_limit_bytes=10 * 2**20),
        cost_estimate=pl.CostEstimate(flops=flops, bytes_accessed=2**20, transcendentals=0),
        name=name,
    )(*args)


def swap_with(value, axis, partner):
    size = lax.axis_size(axis)
    pairs = [(i, partner(i)) for i in range(size) if 0 <= partner(i) < size]
    return lax.ppermute(value, axis, pairs)


def per_device(x, w, close, sharp, table, tally):
    groups, patches, width = x.shape
    breadth = width // sharp.shape[0]
    chips = lax.axis_size("tm") // 2
    block = x.shape
    part = (groups, breadth, HALF)
    x_odd = swap_with(x, "stations", lambda i: i + 2 * (i % 2) - 1)
    x_even = swap_with(x, "stations", lambda i: i ^ 1)
    wide = groups * T
    sums = (groups, patches, 2 * width)
    (means,) = call(means_kernel, breadth, [((HALF, HALF), BF16)], (), name="means")
    k, v, keep, give = call(
        states_kernel, breadth, [(block, BF16)] * 2 + [(part, F32), (part, BF16)], (x, w, means), name="states"
    )
    got = swap_with(give, "tm", lambda i: i ^ 1)
    (total,) = call(combine_kernel, breadth, [(part, BF16)], (keep, got), name="combine")
    pieces = [swap_with(total, "tm", lambda i: i ^ (2 * m)) for m in range(1, chips)]
    q, lin = call(
        own_kernel,
        breadth,
        [(block, BF16), (block, F32)],
        (x, w, means, k, v, total),
        name="own",
        through={5: None},
    )
    (masks,) = call(
        masks_kernel,
        breadth,
        [((3, wide, wide * PAIR // breadth), F32)],
        (table, tally, total),
        name="masks",
        through={2: None},
    )
    (acc,) = call(near_kernel, breadth, [(sums, F32)], (k, v, q, sharp, masks), name="near")
    acc, keep = call(
        even_kernel,
        breadth,
        [(sums, F32), (part, F32)],
        (x_even, w, means, q, sharp, masks, acc, keep),
        [(block, BF16)] * 2,
        name="even",
        through={7: 1},
    )
    send, mine = call(carry_kernel, breadth, [(part, BF16)] * 2, (keep, got, *pieces), name="carry")
    other = swap_with(send, "tm", lambda i: i ^ 1)
    (y,) = call(
        closing_kernel,
        breadth,
        [(block, F32)],
        (q, lin, mine, other, means, close, x),
        [((groups * patches, width), BF16)],
        name="closing",
    )
    (out,) = call(
        odd_kernel,
        breadth,
        [(block, BF16)],
        (x_odd, w, means, q, sharp, masks, acc, close, y),
        [(block, BF16)] * 3,
        name="odd",
    )
    return out


def solution(mesh):
    return jax.shard_map(
        per_device,
        mesh=mesh,
        in_specs=(P("stations", "tm", None), P(), P(), P(), P("stations", None), P("stations")),
        out_specs=P("stations", "tm", None),
        check_vma=False,
    )
```

```python
import functools
import math

import jax
import jax.numpy as jnp
from jax import lax
from jax.experimental import pallas as pl
from jax.experimental.pallas import tpu as pltpu
from jax.sharding import PartitionSpec as P

NEAR = 4
HALF = 256
PAIR = 128
T = 32
F32 = jnp.float32
BF16 = jnp.bfloat16
VMEM = pltpu.VMEM
SMEM = pltpu.SMEM


def dot(a, b):
    return jnp.dot(a, b, preferred_element_type=F32)


def dot_nt(a, b):
    return lax.dot_general(a, b, (((1,), (1,)), ((), ())), preferred_element_type=F32)


def dot_tn(a, b):
    return lax.dot_general(a, b, (((0,), (0,)), ((), ())), preferred_element_type=F32)


def row_norm(x):
    xf = x.astype(F32)
    return (xf * lax.rsqrt(jnp.mean(xf * xf, axis=-1, keepdims=True) + 1e-06)).astype(BF16)


def head_ids(shape, axis, breadth):
    return lax.broadcasted_iota(jnp.int32, shape, axis) // breadth


def means_kernel(breadth, means_ref):
    same = head_ids((HALF, HALF), 0, breadth) == head_ids((HALF, HALF), 1, breadth)
    means_ref[...] = jnp.where(same, 1.0 / breadth, 0.0).astype(BF16)


def head_norm(values, means, epsilon):
    square = (values * values).astype(BF16)
    return (values * lax.rsqrt(dot(square, means) + epsilon)).astype(BF16)


def own_head(values, j, breadth):
    ids = head_ids(values.shape, 1, breadth)
    return jnp.where(ids == j, values, jnp.zeros_like(values))


def pick(low, high, breadth):
    return jnp.where(head_ids(low.shape, 1, breadth) == 0, low, high)


def stack(values, breadth):
    return jnp.concatenate([own_head(values, j, breadth) for j in range(PAIR // breadth)], axis=0)


def cut(ref, c, u):
    groups = ref.shape[0]
    return ref[:, c * T : (c + 1) * T, u * PAIR : (u + 1) * PAIR].reshape(groups * T, PAIR)


def project(normed, w_ref, first, count):
    return [dot(normed, w_ref[:, first + h * HALF : first + (h + 1) * HALF]) for h in range(count)]


def keys_values(x_ref, w_ref, means_ref, k_ref, v_ref, breadth):
    groups, patches, width = x_ref.shape
    halves = width // HALF
    means = means_ref[...]
    normed = row_norm(x_ref[...].reshape(groups * patches, width))
    keys = project(normed, w_ref, width, halves)
    values = project(normed, w_ref, 2 * width, halves)
    for h in range(halves):
        at = slice(h * HALF, (h + 1) * HALF)
        v_ref[:, :, at] = values[h].astype(BF16).reshape(groups, patches, HALF)
        k_ref[:, :, at] = head_norm(keys[h], means, 1e-06).reshape(groups, patches, HALF)


def staggered(items, *stages):
    held = [{} for _ in stages]
    for i in range(len(items) + len(stages) - 1):
        for s, stage in enumerate(stages):
            if 0 <= i - s < len(items):
                before = (held[s - 1].pop(i - s),) if s else ()
                held[s][i - s] = stage(*before, *items[i - s])


def neighbours(breadth, q_ref, windows, sharp_ref, emit):
    groups, patches, width = q_ref.shape
    wide = groups * T
    heads = PAIR // breadth
    ones = stack(jnp.ones((wide, PAIR), BF16), breadth)
    scale = math.log2(math.e) / math.sqrt(breadth)
    lane = lax.broadcasted_iota(jnp.int32, (1, heads * wide), 1) // wide
    sharps = []
    for u in range(width // PAIR):
        row = jnp.full((1, heads * wide), sharp_ref[u * heads] * scale, F32)
        for j in range(1, heads):
            row = jnp.where(lane == j, sharp_ref[u * heads + j] * scale, row)
        sharps.append(row)
    sums = {}

    def score(u, c, n):
        return dot_nt(cut(q_ref, c, u), stack(cut(windows[n][0], c, u), breadth))

    def share(scores, u, c, n):
        return (jnp.exp2(scores * sharps[u]) * windows[n][2][...]).astype(BF16)

    def gather(shares, u, c, n):
        spread = jnp.concatenate([stack(cut(windows[n][1], c, u), breadth), ones], axis=1)
        part = dot(shares, spread)
        total = sums.pop((u, c)) + part if n else part
        if n + 1 < len(windows):
            sums[(u, c)] = total
        else:
            emit(c, u, total)

    items = [(u, c, n) for u in range(width // PAIR) for c in range(patches // T) for n in range(len(windows))]
    staggered(items, score, share, gather)


def masks_kernel(breadth, table_ref, tally_ref, total_ref, mask_ref):
    groups, slots = table_ref.shape
    wide = groups * T
    station = lax.axis_index("stations")
    around = (station, station ^ 1, station + 2 * (station % 2) - 1)
    position = lax.broadcasted_iota(jnp.int32, (8, wide), 1) // T
    ids = jnp.concatenate([place * groups + position for place in around], axis=1)
    rows = []
    for g in range(groups):
        counts = jnp.zeros(ids.shape, F32)
        for j in range(slots):
            slot = jnp.where(j < tally_ref[g], table_ref[g, j], -(1 << 20))
            counts += jnp.where(ids == slot, 1.0, 0.0)
        rows.append(counts[:1])
    t_row = lax.broadcasted_iota(jnp.int32, (T, wide), 0)
    t_col = lax.broadcasted_iota(jnp.int32, (T, wide), 1) % T
    for n in range(len(around)):
        for g in range(groups):
            block = jnp.where(t_row == t_col, jnp.broadcast_to(rows[g][:, n * wide : (n + 1) * wide], (T, wide)), 0.0)
            for j in range(PAIR // breadth):
                mask_ref[n, g * T : (g + 1) * T, j * wide : (j + 1) * wide] = block


def states_kernel(breadth, x_ref, w_ref, means_ref, k_ref, v_ref, keep_ref, give_ref):
    groups, patches, width = x_ref.shape
    core = lax.axis_index("tm") % 2
    keys_values(x_ref, w_ref, means_ref, k_ref, v_ref, breadth)
    for h in range(width // HALF):
        states = []
        for g in range(groups):
            pairs = []
            for u in range(h * HALF // PAIR, (h + 1) * HALF // PAIR):
                at = slice(u * PAIR, (u + 1) * PAIR)
                full = dot_tn(k_ref[g, :, at], v_ref[g, :, at])
                pairs.append(pick(full[:breadth], full[breadth:], breadth))
            states.append(jnp.concatenate(pairs, axis=1))

        @pl.when(core == h)
        def _():
            for g in range(groups):
                keep_ref[g] = states[g]

        @pl.when(core != h)
        def _():
            for g in range(groups):
                give_ref[g] = states[g].astype(BF16)


def own_kernel(breadth, x_ref, w_ref, means_ref, k_ref, v_ref, total_ref, q_ref, lin_ref):
    groups, patches, width = x_ref.shape
    halves = width // HALF
    means = means_ref[...]
    wide = (patches, patches * (PAIR // breadth))
    causal = lax.broadcasted_iota(jnp.int32, wide, 0) >= lax.broadcasted_iota(jnp.int32, wide, 1) % patches
    queries = project(row_norm(x_ref[...].reshape(groups * patches, width)), w_ref, 0, halves)
    for h in range(halves):
        q = head_norm(queries[h], means, 1e-06)
        q_ref[:, :, h * HALF : (h + 1) * HALF] = q.reshape(groups, patches, HALF)

    def score(h, g):
        scores = []
        for u in range(h * HALF // PAIR, (h + 1) * HALF // PAIR):
            at = slice(u * PAIR, (u + 1) * PAIR)
            scores.append(dot_nt(q_ref[g, :, at], stack(k_ref[g, :, at], breadth)))
        return scores

    def share(scores, h, g):
        return jnp.concatenate([jnp.where(causal, s, 0.0).astype(BF16) for s in scores], axis=1)

    def gather(shares, h, g):
        at = slice(h * HALF, (h + 1) * HALF)
        v = v_ref[g, :, at]
        spread = jnp.concatenate([own_head(v, j, breadth) for j in range(HALF // breadth)], axis=0)
        lin_ref[g, :, at] = dot(shares, spread)

    staggered([(h, g) for h in range(halves) for g in range(groups)], score, share, gather)


def near_kernel(breadth, k_ref, v_ref, q_ref, sharp_ref, mask_ref, acc_ref):
    groups = q_ref.shape[0]

    def emit(c, u, total):
        acc_ref[:, c * T : (c + 1) * T, u * 2 * PAIR : (u + 1) * 2 * PAIR] = total.reshape(groups, T, 2 * PAIR)

    neighbours(breadth, q_ref, [(k_ref, v_ref, mask_ref.at[0])], sharp_ref, emit)


def even_kernel(breadth, x_ref, w_ref, means_ref, q_ref, sharp_ref, mask_ref, acc_ref, keep_ref, sum_ref, kept_ref, k_ref, v_ref):
    groups = x_ref.shape[0]
    keys_values(x_ref, w_ref, means_ref, k_ref, v_ref, breadth)

    def emit(c, u, total):
        at = (slice(None), slice(c * T, (c + 1) * T), slice(u * 2 * PAIR, (u + 1) * 2 * PAIR))
        sum_ref[at] = acc_ref[at] + total.reshape(groups, T, 2 * PAIR)

    neighbours(breadth, q_ref, [(k_ref, v_ref, mask_ref.at[1])], sharp_ref, emit)


def odd_kernel(breadth, x_ref, w_ref, means_ref, q_ref, sharp_ref, mask_ref, acc_ref, gathered_ref, k_ref, v_ref):
    groups, patches, width = x_ref.shape
    station = lax.axis_index("stations")
    partner = station + 2 * (station % 2) - 1
    there = (partner >= 0) & (partner < lax.axis_size("stations"))

    def part(c, u):
        return (slice(None), slice(c * T, (c + 1) * T), slice(u * 2 * PAIR, (u + 1) * 2 * PAIR))

    def finish(c, u, total):
        share, weight = total[:, :, :PAIR], total[:, :, PAIR:]
        near = pl.reciprocal(weight, approx=True)
        share = share * (near * (2.0 - weight * near))
        gathered_ref[:, c * T : (c + 1) * T, u * PAIR : (u + 1) * PAIR] = share.astype(BF16)

    @pl.when(there)
    def _():
        keys_values(x_ref, w_ref, means_ref, k_ref, v_ref, breadth)

        def emit(c, u, total):
            finish(c, u, acc_ref[part(c, u)] + total.reshape(groups, T, 2 * PAIR))

        neighbours(breadth, q_ref, [(k_ref, v_ref, mask_ref.at[2])], sharp_ref, emit)

    @pl.when(jnp.logical_not(there))
    def _():
        for u in range(width // PAIR):
            for c in range(patches // T):
                finish(c, u, acc_ref[part(c, u)])


def closing_kernel(breadth, q_ref, lin_ref, mine_ref, other_ref, means_ref, close_ref, x_ref, gathered_ref, out_ref):
    groups, patches, width = q_ref.shape
    rows = groups * patches
    heads = HALF // breadth
    halves = width // HALF
    core = lax.axis_index("tm") % 2
    means = means_ref[...]
    mixed = dot(gathered_ref[...].reshape(rows, width), close_ref[width:, :])
    totals = []
    for h in range(halves):
        at = slice(h * HALF, (h + 1) * HALF)
        for g in range(groups):
            state = jnp.where(core == h, mine_ref[g], other_ref[g])
            block = jnp.where(means > 0, jnp.concatenate([state] * heads, axis=0), jnp.zeros((), BF16))
            totals.append(lin_ref[g, :, at] + dot(q_ref[g, :, at], block))
    for h in range(halves):
        total = jnp.concatenate(totals[h * groups : (h + 1) * groups], axis=0)
        mixed += dot(head_norm(total, means, 1e-05), close_ref[h * HALF : (h + 1) * HALF, :])
    out_ref[...] = (x_ref[...].astype(F32) + mixed.reshape(groups, patches, width)).astype(BF16)


def combine_kernel(breadth, keep_ref, got_ref, total_ref):
    total_ref[...] = (keep_ref[...] + got_ref[...].astype(F32)).astype(BF16)


def carry_kernel(breadth, keep_ref, got_ref, *refs):
    *pieces, send_ref, mine_ref = refs
    core, chip = lax.axis_index("tm") % 2, lax.axis_index("tm") // 2
    before = jnp.zeros(keep_ref.shape, F32)
    for m, piece in enumerate(pieces, 1):
        before += jnp.where((chip ^ m) < chip, piece[...].astype(F32), 0.0)
    send_ref[...] = (before + jnp.where(core == 0, keep_ref[...], 0.0)).astype(BF16)
    mine_ref[...] = (before + jnp.where(core == 0, 0.0, got_ref[...].astype(F32))).astype(BF16)


def call(kernel, breadth, outs, args, scratch=(), flops=10**6, name=None, through=None):
    def place(a):
        return pl.BlockSpec(memory_space=SMEM if a.size <= 64 else VMEM)

    in_specs, out_specs = [place(a) for a in args], [pl.BlockSpec(memory_space=VMEM) for _ in outs]
    for i, o in (through or {}).items():
        in_specs[i] = pl.BlockSpec(memory_space=pl.ANY)
        if o is not None:
            out_specs[o] = in_specs[i]
    return pl.pallas_call(
        functools.partial(kernel, breadth),
        out_shape=[jax.ShapeDtypeStruct(s, d) for s, d in outs],
        in_specs=in_specs,
        out_specs=out_specs,
        scratch_shapes=[pltpu.VMEM(s, d) for s, d in scratch],
        input_output_aliases={i: o for i, o in (through or {}).items() if o is not None},
        compiler_params=pltpu.CompilerParams(vmem_limit_bytes=10 * 2**20),
        cost_estimate=pl.CostEstimate(flops=flops, bytes_accessed=2**20, transcendentals=0),
        name=name,
    )(*args)


def swap_with(value, axis, partner):
    size = lax.axis_size(axis)
    pairs = [(i, partner(i)) for i in range(size) if 0 <= partner(i) < size]
    return lax.ppermute(value, axis, pairs)


def per_device(x, w, close, sharp, table, tally):
    groups, patches, width = x.shape
    breadth = width // sharp.shape[0]
    chips = lax.axis_size("tm") // 2
    block = x.shape
    part = (groups, breadth, HALF)
    x_odd = swap_with(x, "stations", lambda i: i + 2 * (i % 2) - 1)
    x_even = swap_with(x, "stations", lambda i: i ^ 1)
    wide = groups * T
    sums = (groups, patches, 2 * width)
    (means,) = call(means_kernel, breadth, [((HALF, HALF), BF16)], (), name="means", flops=10**10)
    k, v, keep, give = call(
        states_kernel, breadth, [(block, BF16)] * 2 + [(part, F32), (part, BF16)], (x, w, means), name="states"
    )
    got = swap_with(give, "tm", lambda i: i ^ 1)
    (total,) = call(combine_kernel, breadth, [(part, BF16)], (keep, got), name="combine")
    pieces = [swap_with(total, "tm", lambda i: i ^ (2 * m)) for m in range(1, chips)]
    q, lin = call(
        own_kernel,
        breadth,
        [(block, BF16), (block, F32)],
        (x, w, means, k, v, total),
        name="own",
        through={5: None},
    )
    (masks,) = call(
        masks_kernel,
        breadth,
        [((3, wide, wide * PAIR // breadth), F32)],
        (table, tally, total),
        name="masks",
        through={2: None},
    )
    (acc,) = call(near_kernel, breadth, [(sums, F32)], (k, v, q, sharp, masks), name="near")
    acc, keep = call(
        even_kernel,
        breadth,
        [(sums, F32), (part, F32)],
        (x_even, w, means, q, sharp, masks, acc, keep),
        [(block, BF16)] * 2,
        name="even",
        through={7: 1},
    )
    send, mine = call(carry_kernel, breadth, [(part, BF16)] * 2, (keep, got, *pieces), name="carry")
    other = swap_with(send, "tm", lambda i: i ^ 1)
    (gathered,) = call(
        odd_kernel,
        breadth,
        [(block, BF16)],
        (x_odd, w, means, q, sharp, masks, acc),
        [(block, BF16)] * 2,
        name="odd",
    )
    (out,) = call(
        closing_kernel, breadth, [(block, BF16)], (q, lin, mine, other, means, close, x, gathered), name="closing"
    )
    return out


def solution(mesh):
    return jax.shard_map(
        per_device,
        mesh=mesh,
        in_specs=(P("stations", "tm", None), P(), P(), P(), P("stations", None), P("stations")),
        out_specs=P("stations", "tm", None),
        check_vma=False,
    )
```

```python
import functools
import math

import jax
import jax.numpy as jnp
from jax import lax
from jax.experimental import pallas as pl
from jax.experimental.pallas import tpu as pltpu
from jax.sharding import PartitionSpec as P

NEAR = 4
HALF = 256
PAIR = 128
T = 32
F32 = jnp.float32
BF16 = jnp.bfloat16
VMEM = pltpu.VMEM


def dot(a, b):
    return jnp.dot(a, b, preferred_element_type=F32)


def dot_nt(a, b):
    return lax.dot_general(a, b, (((1,), (1,)), ((), ())), preferred_element_type=F32)


def dot_tn(a, b):
    return lax.dot_general(a, b, (((0,), (0,)), ((), ())), preferred_element_type=F32)


def row_norm(x):
    xf = x.astype(F32)
    return (xf * lax.rsqrt(jnp.mean(xf * xf, axis=-1, keepdims=True) + 1e-06)).astype(BF16)


def head_ids(shape, axis, breadth):
    return lax.broadcasted_iota(jnp.int32, shape, axis) // breadth


def means_kernel(breadth, means_ref):
    same = head_ids((HALF, HALF), 0, breadth) == head_ids((HALF, HALF), 1, breadth)
    means_ref[...] = jnp.where(same, 1.0 / breadth, 0.0).astype(BF16)


def head_norm(values, means, epsilon):
    square = (values * values).astype(BF16)
    return (values * lax.rsqrt(dot(square, means) + epsilon)).astype(BF16)


def own_head(values, j, breadth):
    ids = head_ids(values.shape, 1, breadth)
    return jnp.where(ids == j, values, jnp.zeros_like(values))


def pick(low, high, breadth):
    return jnp.where(head_ids(low.shape, 1, breadth) == 0, low, high)


def stack(values, breadth):
    return jnp.concatenate([own_head(values, j, breadth) for j in range(PAIR // breadth)], axis=0)


def cut(ref, c, u):
    groups = ref.shape[0]
    return ref[:, c * T : (c + 1) * T, u * PAIR : (u + 1) * PAIR].reshape(groups * T, PAIR)


def project(normed, w_ref, first, count):
    return [dot(normed, w_ref[:, first + h * HALF : first + (h + 1) * HALF]) for h in range(count)]


def keys_values(x_ref, w_ref, means_ref, k_ref, v_ref, breadth):
    groups, patches, width = x_ref.shape
    halves = width // HALF
    means = means_ref[...]
    normed = row_norm(x_ref[...].reshape(groups * patches, width))
    keys = project(normed, w_ref, width, halves)
    values = project(normed, w_ref, 2 * width, halves)
    for h in range(halves):
        at = slice(h * HALF, (h + 1) * HALF)
        v_ref[:, :, at] = values[h].astype(BF16).reshape(groups, patches, HALF)
        k_ref[:, :, at] = head_norm(keys[h], means, 1e-06).reshape(groups, patches, HALF)


def staggered(items, *stages):
    held = [{} for _ in stages]
    for i in range(len(items) + len(stages) - 1):
        for s, stage in enumerate(stages):
            if 0 <= i - s < len(items):
                before = (held[s - 1].pop(i - s),) if s else ()
                held[s][i - s] = stage(*before, *items[i - s])


def neighbours(breadth, q_ref, windows, row_ref, emit):
    groups, patches, width = q_ref.shape
    wide = groups * T
    ones = stack(jnp.ones((wide, PAIR), BF16), breadth)
    sums = {}

    def score(u, c, n):
        return dot_nt(cut(q_ref, c, u), stack(cut(windows[n][0], c, u), breadth))

    def share(scores, u, c, n):
        return (jnp.exp2(scores * row_ref[u : u + 1, :]) * windows[n][2][...]).astype(BF16)

    def gather(shares, u, c, n):
        spread = jnp.concatenate([stack(cut(windows[n][1], c, u), breadth), ones], axis=1)
        part = dot(shares, spread)
        total = sums.pop((u, c)) + part if n else part
        if n + 1 < len(windows):
            sums[(u, c)] = total
        else:
            emit(c, u, total)

    items = [(u, c, n) for u in range(width // PAIR) for c in range(patches // T) for n in range(len(windows))]
    staggered(items, score, share, gather)


def masks_kernel(breadth, table_ref, tally_ref, sharp_ref, total_ref, mask_ref, row_ref):
    groups, slots = table_ref.shape
    wide = groups * T
    heads = PAIR // breadth
    scale = math.log2(math.e) / math.sqrt(breadth)
    lane = lax.broadcasted_iota(jnp.int32, (1, heads * wide), 1) // wide
    for u in range(row_ref.shape[0]):
        row = jnp.zeros(lane.shape, F32)
        for j in range(heads):
            row = jnp.where(lane == j, sharp_ref[:, u * heads + j : u * heads + j + 1], row)
        row_ref[u : u + 1, :] = row * scale
    station = lax.axis_index("stations")
    around = (station, station ^ 1, station + 2 * (station % 2) - 1)
    position = lax.broadcasted_iota(jnp.int32, (1, wide), 1) // T
    ids = jnp.concatenate([place * groups + position for place in around], axis=1)
    rows = []
    for g in range(groups):
        counts = jnp.zeros(ids.shape, F32)
        for j in range(slots):
            slot = jnp.where(tally_ref[:, g : g + 1] > j, table_ref[g : g + 1, j : j + 1], -(1 << 20))
            counts += jnp.where(ids == slot, 1.0, 0.0)
        rows.append(counts)
    t_row = lax.broadcasted_iota(jnp.int32, (T, wide), 0)
    t_col = lax.broadcasted_iota(jnp.int32, (T, wide), 1) % T
    for n in range(len(around)):
        for g in range(groups):
            block = jnp.where(t_row == t_col, jnp.broadcast_to(rows[g][:, n * wide : (n + 1) * wide], (T, wide)), 0.0)
            for j in range(heads):
                mask_ref[n, g * T : (g + 1) * T, j * wide : (j + 1) * wide] = block


def states_kernel(breadth, x_ref, w_ref, means_ref, k_ref, v_ref, keep_ref, give_ref):
    groups, patches, width = x_ref.shape
    core = lax.axis_index("tm") % 2
    keys_values(x_ref, w_ref, means_ref, k_ref, v_ref, breadth)
    for h in range(width // HALF):
        states = []
        for g in range(groups):
            pairs = []
            for u in range(h * HALF // PAIR, (h + 1) * HALF // PAIR):
                at = slice(u * PAIR, (u + 1) * PAIR)
                full = dot_tn(k_ref[g, :, at], v_ref[g, :, at])
                pairs.append(pick(full[:breadth], full[breadth:], breadth))
            states.append(jnp.concatenate(pairs, axis=1))

        @pl.when(core == h)
        def _():
            for g in range(groups):
                keep_ref[g] = states[g]

        @pl.when(core != h)
        def _():
            for g in range(groups):
                give_ref[g] = states[g].astype(BF16)


def own_kernel(breadth, x_ref, w_ref, means_ref, k_ref, v_ref, q_ref, lin_ref):
    groups, patches, width = x_ref.shape
    halves = width // HALF
    means = means_ref[...]
    wide = (patches, patches * (PAIR // breadth))
    causal = lax.broadcasted_iota(jnp.int32, wide, 0) >= lax.broadcasted_iota(jnp.int32, wide, 1) % patches
    queries = project(row_norm(x_ref[...].reshape(groups * patches, width)), w_ref, 0, halves)
    for h in range(halves):
        q = head_norm(queries[h], means, 1e-06)
        q_ref[:, :, h * HALF : (h + 1) * HALF] = q.reshape(groups, patches, HALF)

    def score(h, g):
        scores = []
        for u in range(h * HALF // PAIR, (h + 1) * HALF // PAIR):
            at = slice(u * PAIR, (u + 1) * PAIR)
            scores.append(dot_nt(q_ref[g, :, at], stack(k_ref[g, :, at], breadth)))
        return scores

    def share(scores, h, g):
        return jnp.concatenate([jnp.where(causal, s, 0.0).astype(BF16) for s in scores], axis=1)

    def gather(shares, h, g):
        at = slice(h * HALF, (h + 1) * HALF)
        v = v_ref[g, :, at]
        spread = jnp.concatenate([own_head(v, j, breadth) for j in range(HALF // breadth)], axis=0)
        lin_ref[g, :, at] = dot(shares, spread)

    staggered([(h, g) for h in range(halves) for g in range(groups)], score, share, gather)


def near_kernel(breadth, k_ref, v_ref, q_ref, row_ref, mask_ref, acc_ref):
    groups = q_ref.shape[0]

    def emit(c, u, total):
        acc_ref[:, c * T : (c + 1) * T, u * 2 * PAIR : (u + 1) * 2 * PAIR] = total.reshape(groups, T, 2 * PAIR)

    neighbours(breadth, q_ref, [(k_ref, v_ref, mask_ref.at[0])], row_ref, emit)


def even_kernel(breadth, x_ref, w_ref, means_ref, q_ref, row_ref, mask_ref, acc_ref, keep_ref, sum_ref, kept_ref, k_ref, v_ref):
    groups = x_ref.shape[0]
    keys_values(x_ref, w_ref, means_ref, k_ref, v_ref, breadth)

    def emit(c, u, total):
        at = (slice(None), slice(c * T, (c + 1) * T), slice(u * 2 * PAIR, (u + 1) * 2 * PAIR))
        sum_ref[at] = acc_ref[at] + total.reshape(groups, T, 2 * PAIR)

    neighbours(breadth, q_ref, [(k_ref, v_ref, mask_ref.at[1])], row_ref, emit)


def odd_kernel(breadth, x_ref, w_ref, means_ref, q_ref, row_ref, mask_ref, acc_ref, gathered_ref, k_ref, v_ref):
    groups, patches, width = x_ref.shape
    station = lax.axis_index("stations")
    partner = station + 2 * (station % 2) - 1
    there = (partner >= 0) & (partner < lax.axis_size("stations"))

    def part(c, u):
        return (slice(None), slice(c * T, (c + 1) * T), slice(u * 2 * PAIR, (u + 1) * 2 * PAIR))

    def finish(c, u, total):
        share, weight = total[:, :, :PAIR], total[:, :, PAIR:]
        near = pl.reciprocal(weight, approx=True)
        share = share * (near * (2.0 - weight * near))
        gathered_ref[:, c * T : (c + 1) * T, u * PAIR : (u + 1) * PAIR] = share.astype(BF16)

    @pl.when(there)
    def _():
        keys_values(x_ref, w_ref, means_ref, k_ref, v_ref, breadth)

        def emit(c, u, total):
            finish(c, u, acc_ref[part(c, u)] + total.reshape(groups, T, 2 * PAIR))

        neighbours(breadth, q_ref, [(k_ref, v_ref, mask_ref.at[2])], row_ref, emit)

    @pl.when(jnp.logical_not(there))
    def _():
        for u in range(width // PAIR):
            for c in range(patches // T):
                finish(c, u, acc_ref[part(c, u)])


def closing_kernel(breadth, q_ref, lin_ref, mine_ref, other_ref, means_ref, close_ref, x_ref, gathered_ref, out_hbm, out_ref, sem):
    groups, patches, width = q_ref.shape
    heads = HALF // breadth
    core = lax.axis_index("tm") % 2
    means = means_ref[...]
    copies = [pltpu.make_async_copy(out_ref.at[g], out_hbm.at[g], sem.at[g]) for g in range(groups)]

    def totals(g):
        both = []
        for h in range(width // HALF):
            at = slice(h * HALF, (h + 1) * HALF)
            state = jnp.where(core == h, mine_ref[g], other_ref[g])
            block = jnp.where(means > 0, jnp.concatenate([state] * heads, axis=0), jnp.zeros((), BF16))
            both.append(lin_ref[g, :, at] + dot(q_ref[g, :, at], block))
        return both

    def squares(both, g):
        return both, [dot((t * t).astype(BF16), means) for t in both]

    def normalize(pair, g):
        return [(t * lax.rsqrt(m + 1e-05)).astype(BF16) for t, m in zip(*pair)]

    def output(parts, g):
        mixed = dot(jnp.concatenate(parts + [gathered_ref[g]], axis=1), close_ref[...])
        out_ref[g] = (x_ref[g].astype(F32) + mixed).astype(BF16)
        copies[g].start()

    staggered([(g,) for g in range(groups)], totals, squares, normalize, output)
    for copy in copies:
        copy.wait()


def combine_kernel(breadth, keep_ref, got_ref, q_ref, total_ref):
    total_ref[...] = (keep_ref[...] + got_ref[...].astype(F32)).astype(BF16)


def carry_kernel(breadth, keep_ref, got_ref, *refs):
    *pieces, send_ref, mine_ref = refs
    core, chip = lax.axis_index("tm") % 2, lax.axis_index("tm") // 2
    before = jnp.zeros(keep_ref.shape, F32)
    for m, piece in enumerate(pieces, 1):
        before += jnp.where((chip ^ m) < chip, piece[...].astype(F32), 0.0)
    send_ref[...] = (before + jnp.where(core == 0, keep_ref[...], 0.0)).astype(BF16)
    mine_ref[...] = (before + jnp.where(core == 0, 0.0, got_ref[...].astype(F32))).astype(BF16)


def call(kernel, breadth, outs, args, scratch=(), flops=10**6, name=None, through=None, space=VMEM):
    in_specs = [pl.BlockSpec(memory_space=VMEM) for _ in args]
    out_specs = [pl.BlockSpec(memory_space=space) for _ in outs]
    for i, o in (through or {}).items():
        in_specs[i] = pl.BlockSpec(memory_space=pl.ANY)
        if o is not None:
            out_specs[o] = in_specs[i]
    return pl.pallas_call(
        functools.partial(kernel, breadth),
        out_shape=[jax.ShapeDtypeStruct(s, d) for s, d in outs],
        in_specs=in_specs,
        out_specs=out_specs,
        scratch_shapes=[pltpu.VMEM(*s) if isinstance(s, tuple) else s for s in scratch],
        input_output_aliases={i: o for i, o in (through or {}).items() if o is not None},
        compiler_params=pltpu.CompilerParams(vmem_limit_bytes=10 * 2**20),
        cost_estimate=pl.CostEstimate(flops=flops, bytes_accessed=2**20, transcendentals=0),
        name=name,
    )(*args)


def swap_with(value, axis, partner):
    size = lax.axis_size(axis)
    pairs = [(i, partner(i)) for i in range(size) if 0 <= partner(i) < size]
    return lax.ppermute(value, axis, pairs)


def per_device(x, w, close, sharp, table, tally):
    groups, patches, width = x.shape
    breadth = width // sharp.shape[0]
    chips = lax.axis_size("tm") // 2
    block = x.shape
    part = (groups, breadth, HALF)
    x_odd = swap_with(x, "stations", lambda i: i + 2 * (i % 2) - 1)
    x_even = swap_with(x, "stations", lambda i: i ^ 1)
    wide = groups * T
    sums = (groups, patches, 2 * width)
    (means,) = call(means_kernel, breadth, [((HALF, HALF), BF16)], (), name="means", flops=10**10)
    k, v, keep, give = call(
        states_kernel, breadth, [(block, BF16)] * 2 + [(part, F32), (part, BF16)], (x, w, means), name="states"
    )
    got = swap_with(give, "tm", lambda i: i ^ 1)
    q, lin = call(
        own_kernel,
        breadth,
        [(block, BF16), (block, F32)],
        (x, w, means, k, v),
        name="own",
    )
    (total,) = call(combine_kernel, breadth, [(part, BF16)], (keep, got, q), name="combine", through={2: None})
    pieces = [swap_with(total, "tm", lambda i: i ^ (2 * m)) for m in range(1, chips)]
    masks, rows = call(
        masks_kernel,
        breadth,
        [((3, wide, wide * PAIR // breadth), F32), ((width // PAIR, wide * PAIR // breadth), F32)],
        (table, tally.reshape(1, -1), sharp.reshape(1, -1), total),
        name="masks",
        through={3: None},
    )
    (acc,) = call(near_kernel, breadth, [(sums, F32)], (k, v, q, rows, masks), name="near")
    acc, keep = call(
        even_kernel,
        breadth,
        [(sums, F32), (part, F32)],
        (x_even, w, means, q, rows, masks, acc, keep),
        [(block, BF16)] * 2,
        name="even",
        through={7: 1},
    )
    send, mine = call(carry_kernel, breadth, [(part, BF16)] * 2, (keep, got, *pieces), name="carry")
    other = swap_with(send, "tm", lambda i: i ^ 1)
    (gathered,) = call(
        odd_kernel,
        breadth,
        [(block, BF16)],
        (x_odd, w, means, q, rows, masks, acc),
        [(block, BF16)] * 2,
        name="odd",
    )
    (out,) = call(
        closing_kernel,
        breadth,
        [(block, BF16)],
        (q, lin, mine, other, means, close, x, gathered),
        [(block, BF16), pltpu.SemaphoreType.DMA((groups,))],
        name="closing",
        space=pl.ANY,
    )
    return out


def solution(mesh):
    return jax.shard_map(
        per_device,
        mesh=mesh,
        in_specs=(P("stations", "tm", None), P(), P(), P(), P("stations", None), P("stations")),
        out_specs=P("stations", "tm", None),
        check_vma=False,
    )
```

```python
import functools
import math

import jax
import jax.numpy as jnp
from jax import lax
from jax.experimental import pallas as pl
from jax.experimental.pallas import tpu as pltpu
from jax.sharding import PartitionSpec as P

NEAR = 4
HALF = 256
PAIR = 128
T = 32
F32 = jnp.float32
BF16 = jnp.bfloat16
VMEM = pltpu.VMEM


def dot(a, b):
    return jnp.dot(a, b, preferred_element_type=F32)


def dot_nt(a, b):
    return lax.dot_general(a, b, (((1,), (1,)), ((), ())), preferred_element_type=F32)


def dot_tn(a, b):
    return lax.dot_general(a, b, (((0,), (0,)), ((), ())), preferred_element_type=F32)


def row_norm(x):
    xf = x.astype(F32)
    return (xf * lax.rsqrt(jnp.mean(xf * xf, axis=-1, keepdims=True) + 1e-06)).astype(BF16)


def head_ids(shape, axis, breadth):
    return lax.broadcasted_iota(jnp.int32, shape, axis) // breadth


def means_kernel(breadth, means_ref):
    same = head_ids((HALF, HALF), 0, breadth) == head_ids((HALF, HALF), 1, breadth)
    means_ref[...] = jnp.where(same, 1.0 / breadth, 0.0).astype(BF16)


def head_norm(values, means, epsilon):
    square = (values * values).astype(BF16)
    return (values * lax.rsqrt(dot(square, means) + epsilon)).astype(BF16)


def own_head(values, j, breadth):
    ids = head_ids(values.shape, 1, breadth)
    return jnp.where(ids == j, values, jnp.zeros_like(values))


def pick(low, high, breadth):
    return jnp.where(head_ids(low.shape, 1, breadth) == 0, low, high)


def stack(values, breadth):
    return jnp.concatenate([own_head(values, j, breadth) for j in range(PAIR // breadth)], axis=0)


def cut(ref, c, u):
    groups = ref.shape[0]
    return ref[:, c * T : (c + 1) * T, u * PAIR : (u + 1) * PAIR].reshape(groups * T, PAIR)


def project(normed, w_ref, first, count):
    return [dot(normed, w_ref[:, first + h * HALF : first + (h + 1) * HALF]) for h in range(count)]


def keys_values(x_ref, w_ref, means_ref, k_ref, v_ref, breadth):
    groups, patches, width = x_ref.shape
    halves = width // HALF
    means = means_ref[...]
    normed = row_norm(x_ref[...].reshape(groups * patches, width))
    keys = project(normed, w_ref, width, halves)
    values = project(normed, w_ref, 2 * width, halves)
    for h in range(halves):
        at = slice(h * HALF, (h + 1) * HALF)
        v_ref[:, :, at] = values[h].astype(BF16).reshape(groups, patches, HALF)
        k_ref[:, :, at] = head_norm(keys[h], means, 1e-06).reshape(groups, patches, HALF)


def staggered(items, *stages):
    held = [{} for _ in stages]
    for i in range(len(items) + len(stages) - 1):
        for s, stage in enumerate(stages):
            if 0 <= i - s < len(items):
                before = (held[s - 1].pop(i - s),) if s else ()
                held[s][i - s] = stage(*before, *items[i - s])


def neighbours(breadth, q_ref, windows, row_ref, emit):
    groups, patches, width = q_ref.shape
    wide = groups * T
    ones = stack(jnp.ones((wide, PAIR), BF16), breadth)
    sums = {}

    def score(u, c, n):
        return dot_nt(cut(q_ref, c, u), stack(cut(windows[n][0], c, u), breadth))

    def share(scores, u, c, n):
        return (jnp.exp2(scores * row_ref[u : u + 1, :]) * windows[n][2][...]).astype(BF16)

    def gather(shares, u, c, n):
        spread = jnp.concatenate([stack(cut(windows[n][1], c, u), breadth), ones], axis=1)
        part = dot(shares, spread)
        total = sums.pop((u, c)) + part if n else part
        if n + 1 < len(windows):
            sums[(u, c)] = total
        else:
            emit(c, u, total)

    items = [(u, c, n) for u in range(width // PAIR) for c in range(patches // T) for n in range(len(windows))]
    staggered(items, score, share, gather)


def masks_kernel(breadth, table_ref, tally_ref, sharp_ref, total_ref, mask_ref, row_ref):
    groups, slots = table_ref.shape
    wide = groups * T
    heads = PAIR // breadth
    scale = math.log2(math.e) / math.sqrt(breadth)
    lane = lax.broadcasted_iota(jnp.int32, (1, heads * wide), 1) // wide
    for u in range(row_ref.shape[0]):
        row = jnp.zeros(lane.shape, F32)
        for j in range(heads):
            row = jnp.where(lane == j, sharp_ref[:, u * heads + j : u * heads + j + 1], row)
        row_ref[u : u + 1, :] = row * scale
    station = lax.axis_index("stations")
    around = (station, station ^ 1, station + 2 * (station % 2) - 1)
    position = lax.broadcasted_iota(jnp.int32, (1, wide), 1) // T
    ids = jnp.concatenate([place * groups + position for place in around], axis=1)
    rows = []
    for g in range(groups):
        counts = jnp.zeros(ids.shape, F32)
        for j in range(slots):
            slot = jnp.where(tally_ref[:, g : g + 1] > j, table_ref[g : g + 1, j : j + 1], -(1 << 20))
            counts += jnp.where(ids == slot, 1.0, 0.0)
        rows.append(counts)
    t_row = lax.broadcasted_iota(jnp.int32, (T, wide), 0)
    t_col = lax.broadcasted_iota(jnp.int32, (T, wide), 1) % T
    for n in range(len(around)):
        for g in range(groups):
            block = jnp.where(t_row == t_col, jnp.broadcast_to(rows[g][:, n * wide : (n + 1) * wide], (T, wide)), 0.0)
            for j in range(heads):
                mask_ref[n, g * T : (g + 1) * T, j * wide : (j + 1) * wide] = block


def states_kernel(breadth, x_ref, w_ref, means_ref, k_ref, v_ref, keep_ref, give_ref):
    groups, patches, width = x_ref.shape
    core = lax.axis_index("tm") % 2
    keys_values(x_ref, w_ref, means_ref, k_ref, v_ref, breadth)
    for h in range(width // HALF):
        states = []
        for g in range(groups):
            pairs = []
            for u in range(h * HALF // PAIR, (h + 1) * HALF // PAIR):
                at = slice(u * PAIR, (u + 1) * PAIR)
                full = dot_tn(k_ref[g, :, at], v_ref[g, :, at])
                pairs.append(pick(full[:breadth], full[breadth:], breadth))
            states.append(jnp.concatenate(pairs, axis=1))

        @pl.when(core == h)
        def _():
            for g in range(groups):
                keep_ref[g] = states[g]

        @pl.when(core != h)
        def _():
            for g in range(groups):
                give_ref[g] = states[g].astype(BF16)


def own_kernel(breadth, x_ref, w_ref, means_ref, k_ref, v_ref, total_ref, q_ref, lin_ref):
    groups, patches, width = x_ref.shape
    halves = width // HALF
    means = means_ref[...]
    wide = (patches, patches * (PAIR // breadth))
    causal = lax.broadcasted_iota(jnp.int32, wide, 0) >= lax.broadcasted_iota(jnp.int32, wide, 1) % patches
    queries = project(row_norm(x_ref[...].reshape(groups * patches, width)), w_ref, 0, halves)
    for h in range(halves):
        q = head_norm(queries[h], means, 1e-06)
        q_ref[:, :, h * HALF : (h + 1) * HALF] = q.reshape(groups, patches, HALF)

    def score(h, g):
        scores = []
        for u in range(h * HALF // PAIR, (h + 1) * HALF // PAIR):
            at = slice(u * PAIR, (u + 1) * PAIR)
            scores.append(dot_nt(q_ref[g, :, at], stack(k_ref[g, :, at], breadth)))
        return scores

    def share(scores, h, g):
        return jnp.concatenate([jnp.where(causal, s, 0.0).astype(BF16) for s in scores], axis=1)

    def gather(shares, h, g):
        at = slice(h * HALF, (h + 1) * HALF)
        v = v_ref[g, :, at]
        spread = jnp.concatenate([own_head(v, j, breadth) for j in range(HALF // breadth)], axis=0)
        lin_ref[g, :, at] = dot(shares, spread)

    staggered([(h, g) for h in range(halves) for g in range(groups)], score, share, gather)


def near_kernel(breadth, k_ref, v_ref, q_ref, row_ref, mask_ref, acc_ref):
    groups = q_ref.shape[0]

    def emit(c, u, total):
        acc_ref[:, c * T : (c + 1) * T, u * 2 * PAIR : (u + 1) * 2 * PAIR] = total.reshape(groups, T, 2 * PAIR)

    neighbours(breadth, q_ref, [(k_ref, v_ref, mask_ref.at[0])], row_ref, emit)


def even_kernel(breadth, x_ref, w_ref, means_ref, q_ref, row_ref, mask_ref, acc_ref, keep_ref, sum_ref, kept_ref, k_ref, v_ref):
    groups = x_ref.shape[0]
    keys_values(x_ref, w_ref, means_ref, k_ref, v_ref, breadth)

    def emit(c, u, total):
        at = (slice(None), slice(c * T, (c + 1) * T), slice(u * 2 * PAIR, (u + 1) * 2 * PAIR))
        sum_ref[at] = acc_ref[at] + total.reshape(groups, T, 2 * PAIR)

    neighbours(breadth, q_ref, [(k_ref, v_ref, mask_ref.at[1])], row_ref, emit)


def odd_partner():
    station = lax.axis_index("stations")
    partner = station + 2 * (station % 2) - 1
    return (partner >= 0) & (partner < lax.axis_size("stations"))


def odd_keys_kernel(breadth, x_ref, w_ref, means_ref, keep_ref, k_ref, v_ref, kept_ref):
    @pl.when(odd_partner())
    def _():
        keys_values(x_ref, w_ref, means_ref, k_ref, v_ref, breadth)


def odd_kernel(breadth, k_ref, v_ref, q_ref, row_ref, mask_ref, acc_ref, gathered_ref):
    groups, patches, width = q_ref.shape
    there = odd_partner()

    def part(c, u):
        return (slice(None), slice(c * T, (c + 1) * T), slice(u * 2 * PAIR, (u + 1) * 2 * PAIR))

    def finish(c, u, total):
        share, weight = total[:, :, :PAIR], total[:, :, PAIR:]
        near = pl.reciprocal(weight, approx=True)
        share = share * (near * (2.0 - weight * near))
        gathered_ref[:, c * T : (c + 1) * T, u * PAIR : (u + 1) * PAIR] = share.astype(BF16)

    @pl.when(there)
    def _():
        def emit(c, u, total):
            finish(c, u, acc_ref[part(c, u)] + total.reshape(groups, T, 2 * PAIR))

        neighbours(breadth, q_ref, [(k_ref, v_ref, mask_ref.at[2])], row_ref, emit)

    @pl.when(jnp.logical_not(there))
    def _():
        for u in range(width // PAIR):
            for c in range(patches // T):
                finish(c, u, acc_ref[part(c, u)])


def closing_kernel(breadth, q_ref, lin_ref, mine_ref, other_ref, means_ref, close_ref, x_ref, gathered_ref, out_hbm, out_ref, sem):
    groups, patches, width = q_ref.shape
    heads = HALF // breadth
    core = lax.axis_index("tm") % 2
    means = means_ref[...]
    copies = [pltpu.make_async_copy(out_ref.at[g], out_hbm.at[g], sem.at[g]) for g in range(groups)]

    def totals(g):
        both = []
        for h in range(width // HALF):
            at = slice(h * HALF, (h + 1) * HALF)
            state = jnp.where(core == h, mine_ref[g], other_ref[g])
            block = jnp.where(means > 0, jnp.concatenate([state] * heads, axis=0), jnp.zeros((), BF16))
            both.append(lin_ref[g, :, at] + dot(q_ref[g, :, at], block))
        return both

    def squares(both, g):
        return both, [dot((t * t).astype(BF16), means) for t in both]

    def normalize(pair, g):
        return [(t * lax.rsqrt(m + 1e-05)).astype(BF16) for t, m in zip(*pair)]

    def output(parts, g):
        mixed = dot(jnp.concatenate(parts + [gathered_ref[g]], axis=1), close_ref[...])
        out_ref[g] = (x_ref[g].astype(F32) + mixed).astype(BF16)
        copies[g].start()

    staggered([(g,) for g in range(groups)], totals, squares, normalize, output)
    for copy in copies:
        copy.wait()


def combine_kernel(breadth, keep_ref, got_ref, total_ref):
    total_ref[...] = (keep_ref[...] + got_ref[...].astype(F32)).astype(BF16)


def carry_kernel(breadth, keep_ref, got_ref, *refs):
    *pieces, send_ref, mine_ref = refs
    core, chip = lax.axis_index("tm") % 2, lax.axis_index("tm") // 2
    before = jnp.zeros(keep_ref.shape, F32)
    for m, piece in enumerate(pieces, 1):
        before += jnp.where((chip ^ m) < chip, piece[...].astype(F32), 0.0)
    send_ref[...] = (before + jnp.where(core == 0, keep_ref[...], 0.0)).astype(BF16)
    mine_ref[...] = (before + jnp.where(core == 0, 0.0, got_ref[...].astype(F32))).astype(BF16)


def call(kernel, breadth, outs, args, scratch=(), flops=10**6, name=None, through=None, space=VMEM):
    in_specs = [pl.BlockSpec(memory_space=VMEM) for _ in args]
    out_specs = [pl.BlockSpec(memory_space=space) for _ in outs]
    for i, o in (through or {}).items():
        in_specs[i] = pl.BlockSpec(memory_space=pl.ANY)
        if o is not None:
            out_specs[o] = in_specs[i]
    return pl.pallas_call(
        functools.partial(kernel, breadth),
        out_shape=[jax.ShapeDtypeStruct(s, d) for s, d in outs],
        in_specs=in_specs,
        out_specs=out_specs,
        scratch_shapes=[pltpu.VMEM(*s) if isinstance(s, tuple) else s for s in scratch],
        input_output_aliases={i: o for i, o in (through or {}).items() if o is not None},
        compiler_params=pltpu.CompilerParams(vmem_limit_bytes=10 * 2**20),
        cost_estimate=pl.CostEstimate(flops=flops, bytes_accessed=2**12, transcendentals=0),
        name=name,
    )(*args)


def swap_with(value, axis, partner):
    size = lax.axis_size(axis)
    pairs = [(i, partner(i)) for i in range(size) if 0 <= partner(i) < size]
    return lax.ppermute(value, axis, pairs)


def per_device(x, w, close, sharp, table, tally):
    groups, patches, width = x.shape
    breadth = width // sharp.shape[0]
    chips = lax.axis_size("tm") // 2
    block = x.shape
    part = (groups, breadth, HALF)
    x_odd = swap_with(x, "stations", lambda i: i + 2 * (i % 2) - 1)
    x_even = swap_with(x, "stations", lambda i: i ^ 1)
    wide = groups * T
    sums = (groups, patches, 2 * width)
    (means,) = call(means_kernel, breadth, [((HALF, HALF), BF16)], (), name="means", flops=10**10)
    k, v, keep, give = call(
        states_kernel, breadth, [(block, BF16)] * 2 + [(part, F32), (part, BF16)], (x, w, means), name="states"
    )
    got = swap_with(give, "tm", lambda i: i ^ 1)
    (total,) = call(combine_kernel, breadth, [(part, BF16)], (keep, got), name="combine")
    pieces = [swap_with(total, "tm", lambda i: i ^ (2 * m)) for m in range(1, chips)]
    q, lin = call(
        own_kernel,
        breadth,
        [(block, BF16), (block, F32)],
        (x, w, means, k, v, total),
        name="own",
        through={5: None},
    )
    masks, rows = call(
        masks_kernel,
        breadth,
        [((3, wide, wide * PAIR // breadth), F32), ((width // PAIR, wide * PAIR // breadth), F32)],
        (table, tally.reshape(1, -1), sharp.reshape(1, -1), total),
        name="masks",
        through={3: None},
    )
    (acc,) = call(near_kernel, breadth, [(sums, F32)], (k, v, q, rows, masks), name="near")
    acc, keep = call(
        even_kernel,
        breadth,
        [(sums, F32), (part, F32)],
        (x_even, w, means, q, rows, masks, acc, keep),
        [(block, BF16)] * 2,
        name="even",
        through={7: 1},
    )
    k_odd, v_odd, keep = call(
        odd_keys_kernel,
        breadth,
        [(block, BF16)] * 2 + [(part, F32)],
        (x_odd, w, means, keep),
        name="keys",
        through={3: 2},
    )
    send, mine = call(carry_kernel, breadth, [(part, BF16)] * 2, (keep, got, *pieces), name="carry")
    other = swap_with(send, "tm", lambda i: i ^ 1)
    (gathered,) = call(odd_kernel, breadth, [(block, BF16)], (k_odd, v_odd, q, rows, masks, acc), name="odd")
    (out,) = call(
        closing_kernel,
        breadth,
        [(block, BF16)],
        (q, lin, mine, other, means, close, x, gathered),
        [(block, BF16), pltpu.SemaphoreType.DMA((groups,))],
        name="closing",
        space=pl.ANY,
    )
    return out


def solution(mesh):
    return jax.shard_map(
        per_device,
        mesh=mesh,
        in_specs=(P("stations", "tm", None), P(), P(), P(), P("stations", None), P("stations")),
        out_specs=P("stations", "tm", None),
        check_vma=False,
    )
```

```python
import functools
import math

import jax
import jax.numpy as jnp
from jax import lax
from jax.experimental import pallas as pl
from jax.experimental.pallas import tpu as pltpu
from jax.sharding import PartitionSpec as P

NEAR = 4
HALF = 256
PAIR = 128
T = 32
F32 = jnp.float32
BF16 = jnp.bfloat16
VMEM = pltpu.VMEM


def dot(a, b):
    return jnp.dot(a, b, preferred_element_type=F32)


def dot_nt(a, b):
    return lax.dot_general(a, b, (((1,), (1,)), ((), ())), preferred_element_type=F32)


def dot_tn(a, b):
    return lax.dot_general(a, b, (((0,), (0,)), ((), ())), preferred_element_type=F32)


def row_scale(x):
    xf = x.astype(F32)
    return lax.rsqrt(jnp.mean(xf * xf, axis=-1, keepdims=True) + 1e-06)


def head_ids(shape, axis, breadth):
    return lax.broadcasted_iota(jnp.int32, shape, axis) // breadth


def means_kernel(breadth, means_ref):
    same = head_ids((HALF, HALF), 0, breadth) == head_ids((HALF, HALF), 1, breadth)
    means_ref[...] = jnp.where(same, 1.0 / breadth, 0.0).astype(BF16)


def head_norm(values, means, epsilon):
    square = (values * values).astype(BF16)
    return (values * lax.rsqrt(dot(square, means) + epsilon)).astype(BF16)


def own_head(values, j, breadth):
    ids = head_ids(values.shape, 1, breadth)
    return jnp.where(ids == j, values, jnp.zeros_like(values))


def pick(low, high, breadth):
    return jnp.where(head_ids(low.shape, 1, breadth) == 0, low, high)


def stack(values, breadth):
    return jnp.concatenate([own_head(values, j, breadth) for j in range(PAIR // breadth)], axis=0)


def cut(ref, c, u):
    groups = ref.shape[0]
    return ref[:, c * T : (c + 1) * T, u * PAIR : (u + 1) * PAIR].reshape(groups * T, PAIR)


def project(rows, w_ref, first, count):
    return [dot(rows, w_ref[:, first + h * HALF : first + (h + 1) * HALF]) for h in range(count)]


def keys_values(x_ref, w_ref, means_ref, k_ref, v_ref, breadth):
    groups, patches, width = x_ref.shape
    halves = width // HALF
    means = means_ref[...]
    rows = x_ref[...].reshape(groups * patches, width)
    keys = project(rows, w_ref, width, halves)
    values = project(rows, w_ref, 2 * width, halves)
    scale = row_scale(rows)
    for h in range(halves):
        at = slice(h * HALF, (h + 1) * HALF)
        v_ref[:, :, at] = (values[h] * scale).astype(BF16).reshape(groups, patches, HALF)
        k_ref[:, :, at] = head_norm(keys[h] * scale, means, 1e-06).reshape(groups, patches, HALF)


def staggered(items, *stages):
    held = [{} for _ in stages]
    for i in range(len(items) + len(stages) - 1):
        for s, stage in enumerate(stages):
            if 0 <= i - s < len(items):
                before = (held[s - 1].pop(i - s),) if s else ()
                held[s][i - s] = stage(*before, *items[i - s])


def neighbours(breadth, q_ref, windows, row_ref, emit):
    groups, patches, width = q_ref.shape
    wide = groups * T
    ones = stack(jnp.ones((wide, PAIR), BF16), breadth)
    sums = {}

    def score(u, c, n):
        return dot_nt(cut(q_ref, c, u), stack(cut(windows[n][0], c, u), breadth))

    def share(scores, u, c, n):
        return (jnp.exp2(scores * row_ref[u : u + 1, :]) * windows[n][2][...]).astype(BF16)

    def gather(shares, u, c, n):
        spread = jnp.concatenate([stack(cut(windows[n][1], c, u), breadth), ones], axis=1)
        part = dot(shares, spread)
        total = sums.pop((u, c)) + part if n else part
        if n + 1 < len(windows):
            sums[(u, c)] = total
        else:
            emit(c, u, total)

    items = [(u, c, n) for u in range(width // PAIR) for c in range(patches // T) for n in range(len(windows))]
    staggered(items, score, share, gather)


def masks_kernel(breadth, table_ref, tally_ref, sharp_ref, total_ref, mask_ref, row_ref):
    groups, slots = table_ref.shape
    wide = groups * T
    heads = PAIR // breadth
    scale = math.log2(math.e) / math.sqrt(breadth)
    lane = lax.broadcasted_iota(jnp.int32, (1, heads * wide), 1) // wide
    for u in range(row_ref.shape[0]):
        row = jnp.zeros(lane.shape, F32)
        for j in range(heads):
            row = jnp.where(lane == j, sharp_ref[:, u * heads + j : u * heads + j + 1], row)
        row_ref[u : u + 1, :] = row * scale
    station = lax.axis_index("stations")
    around = (station, station ^ 1, station + 2 * (station % 2) - 1)
    position = lax.broadcasted_iota(jnp.int32, (1, wide), 1) // T
    ids = jnp.concatenate([place * groups + position for place in around], axis=1)
    rows = []
    for g in range(groups):
        counts = jnp.zeros(ids.shape, F32)
        for j in range(slots):
            slot = jnp.where(tally_ref[:, g : g + 1] > j, table_ref[g : g + 1, j : j + 1], -(1 << 20))
            counts += jnp.where(ids == slot, 1.0, 0.0)
        rows.append(counts)
    t_row = lax.broadcasted_iota(jnp.int32, (T, wide), 0)
    t_col = lax.broadcasted_iota(jnp.int32, (T, wide), 1) % T
    for n in range(len(around)):
        for g in range(groups):
            block = jnp.where(t_row == t_col, jnp.broadcast_to(rows[g][:, n * wide : (n + 1) * wide], (T, wide)), 0.0)
            for j in range(heads):
                mask_ref[n, g * T : (g + 1) * T, j * wide : (j + 1) * wide] = block


def states_kernel(breadth, x_ref, w_ref, means_ref, k_ref, v_ref, keep_ref, give_ref):
    groups, patches, width = x_ref.shape
    core = lax.axis_index("tm") % 2
    keys_values(x_ref, w_ref, means_ref, k_ref, v_ref, breadth)
    for h in range(width // HALF):
        states = []
        for g in range(groups):
            pairs = []
            for u in range(h * HALF // PAIR, (h + 1) * HALF // PAIR):
                at = slice(u * PAIR, (u + 1) * PAIR)
                full = dot_tn(k_ref[g, :, at], v_ref[g, :, at])
                pairs.append(pick(full[:breadth], full[breadth:], breadth))
            states.append(jnp.concatenate(pairs, axis=1))

        @pl.when(core == h)
        def _():
            for g in range(groups):
                keep_ref[g] = states[g]

        @pl.when(core != h)
        def _():
            for g in range(groups):
                give_ref[g] = states[g].astype(BF16)


def own_kernel(breadth, x_ref, w_ref, means_ref, k_ref, v_ref, total_ref, q_ref, lin_ref):
    groups, patches, width = x_ref.shape
    halves = width // HALF
    means = means_ref[...]
    wide = (patches, patches * (PAIR // breadth))
    causal = lax.broadcasted_iota(jnp.int32, wide, 0) >= lax.broadcasted_iota(jnp.int32, wide, 1) % patches
    rows = x_ref[...].reshape(groups * patches, width)
    queries = project(rows, w_ref, 0, halves)
    scale = row_scale(rows)
    for h in range(halves):
        q = head_norm(queries[h] * scale, means, 1e-06)
        q_ref[:, :, h * HALF : (h + 1) * HALF] = q.reshape(groups, patches, HALF)

    def score(h, g):
        scores = []
        for u in range(h * HALF // PAIR, (h + 1) * HALF // PAIR):
            at = slice(u * PAIR, (u + 1) * PAIR)
            scores.append(dot_nt(q_ref[g, :, at], stack(k_ref[g, :, at], breadth)))
        return scores

    def share(scores, h, g):
        return jnp.concatenate([jnp.where(causal, s, 0.0).astype(BF16) for s in scores], axis=1)

    def gather(shares, h, g):
        at = slice(h * HALF, (h + 1) * HALF)
        v = v_ref[g, :, at]
        spread = jnp.concatenate([own_head(v, j, breadth) for j in range(HALF // breadth)], axis=0)
        lin_ref[g, :, at] = dot(shares, spread)

    staggered([(h, g) for h in range(halves) for g in range(groups)], score, share, gather)


def near_kernel(breadth, k_ref, v_ref, q_ref, row_ref, mask_ref, acc_ref):
    groups = q_ref.shape[0]

    def emit(c, u, total):
        acc_ref[:, c * T : (c + 1) * T, u * 2 * PAIR : (u + 1) * 2 * PAIR] = total.reshape(groups, T, 2 * PAIR)

    neighbours(breadth, q_ref, [(k_ref, v_ref, mask_ref.at[0])], row_ref, emit)


def even_kernel(breadth, x_ref, w_ref, means_ref, q_ref, row_ref, mask_ref, acc_ref, keep_ref, sum_ref, kept_ref, k_ref, v_ref):
    groups = x_ref.shape[0]
    keys_values(x_ref, w_ref, means_ref, k_ref, v_ref, breadth)

    def emit(c, u, total):
        at = (slice(None), slice(c * T, (c + 1) * T), slice(u * 2 * PAIR, (u + 1) * 2 * PAIR))
        sum_ref[at] = acc_ref[at] + total.reshape(groups, T, 2 * PAIR)

    neighbours(breadth, q_ref, [(k_ref, v_ref, mask_ref.at[1])], row_ref, emit)


def odd_partner():
    station = lax.axis_index("stations")
    partner = station + 2 * (station % 2) - 1
    return (partner >= 0) & (partner < lax.axis_size("stations"))


def odd_keys_kernel(breadth, x_ref, w_ref, means_ref, keep_ref, close_ref, k_ref, v_ref, kept_ref):
    @pl.when(odd_partner())
    def _():
        keys_values(x_ref, w_ref, means_ref, k_ref, v_ref, breadth)


def odd_kernel(breadth, k_ref, v_ref, q_ref, row_ref, mask_ref, acc_ref, gathered_ref):
    groups, patches, width = q_ref.shape
    there = odd_partner()

    def part(c, u):
        return (slice(None), slice(c * T, (c + 1) * T), slice(u * 2 * PAIR, (u + 1) * 2 * PAIR))

    def finish(c, u, total):
        share, weight = total[:, :, :PAIR], total[:, :, PAIR:]
        near = pl.reciprocal(weight, approx=True)
        share = share * (near * (2.0 - weight * near))
        gathered_ref[:, c * T : (c + 1) * T, u * PAIR : (u + 1) * PAIR] = share.astype(BF16)

    @pl.when(there)
    def _():
        def emit(c, u, total):
            finish(c, u, acc_ref[part(c, u)] + total.reshape(groups, T, 2 * PAIR))

        neighbours(breadth, q_ref, [(k_ref, v_ref, mask_ref.at[2])], row_ref, emit)

    @pl.when(jnp.logical_not(there))
    def _():
        for u in range(width // PAIR):
            for c in range(patches // T):
                finish(c, u, acc_ref[part(c, u)])


def closing_kernel(breadth, q_ref, lin_ref, mine_ref, other_ref, means_ref, close_ref, x_ref, gathered_ref, out_hbm, out_ref, sem):
    groups, patches, width = q_ref.shape
    heads = HALF // breadth
    core = lax.axis_index("tm") % 2
    means = means_ref[...]
    copies = [pltpu.make_async_copy(out_ref.at[g], out_hbm.at[g], sem.at[g]) for g in range(groups)]

    def totals(g):
        both = []
        for h in range(width // HALF):
            at = slice(h * HALF, (h + 1) * HALF)
            state = jnp.where(core == h, mine_ref[g], other_ref[g])
            block = jnp.where(means > 0, jnp.concatenate([state] * heads, axis=0), jnp.zeros((), BF16))
            both.append(lin_ref[g, :, at] + dot(q_ref[g, :, at], block))
        return both

    def squares(both, g):
        return both, [dot((t * t).astype(BF16), means) for t in both]

    def normalize(pair, g):
        return [(t * lax.rsqrt(m + 1e-05)).astype(BF16) for t, m in zip(*pair)]

    def output(parts, g):
        mixed = dot(jnp.concatenate(parts + [gathered_ref[g]], axis=1), close_ref[...])
        out_ref[g] = (x_ref[g].astype(F32) + mixed).astype(BF16)
        copies[g].start()

    staggered([(g,) for g in range(groups)], totals, squares, normalize, output)
    for copy in copies:
        copy.wait()


def combine_kernel(breadth, keep_ref, got_ref, total_ref):
    total_ref[...] = (keep_ref[...] + got_ref[...].astype(F32)).astype(BF16)


def carry_kernel(breadth, keep_ref, got_ref, *refs):
    *pieces, send_ref, mine_ref = refs
    core, chip = lax.axis_index("tm") % 2, lax.axis_index("tm") // 2
    before = jnp.zeros(keep_ref.shape, F32)
    for m, piece in zip(range(len(pieces), 0, -1), pieces):
        before += jnp.where((chip ^ m) < chip, piece[...].astype(F32), 0.0)
    send_ref[...] = (before + jnp.where(core == 0, keep_ref[...], 0.0)).astype(BF16)
    mine_ref[...] = (before + jnp.where(core == 0, 0.0, got_ref[...].astype(F32))).astype(BF16)


def call(kernel, breadth, outs, args, scratch=(), flops=10**6, name=None, through=None, space=VMEM):
    in_specs = [pl.BlockSpec(memory_space=VMEM) for _ in args]
    out_specs = [pl.BlockSpec(memory_space=space) for _ in outs]
    for i, o in (through or {}).items():
        in_specs[i] = pl.BlockSpec(memory_space=pl.ANY)
        if o is not None:
            out_specs[o] = in_specs[i]
    return pl.pallas_call(
        functools.partial(kernel, breadth),
        out_shape=[jax.ShapeDtypeStruct(s, d) for s, d in outs],
        in_specs=in_specs,
        out_specs=out_specs,
        scratch_shapes=[pltpu.VMEM(*s) if isinstance(s, tuple) else s for s in scratch],
        input_output_aliases={i: o for i, o in (through or {}).items() if o is not None},
        compiler_params=pltpu.CompilerParams(vmem_limit_bytes=10 * 2**20),
        cost_estimate=pl.CostEstimate(flops=flops, bytes_accessed=2**12, transcendentals=0),
        name=name,
    )(*args)


def swap_with(value, axis, partner):
    size = lax.axis_size(axis)
    pairs = [(i, partner(i)) for i in range(size) if 0 <= partner(i) < size]
    return lax.ppermute(value, axis, pairs)


def per_device(x, w, close, sharp, table, tally):
    groups, patches, width = x.shape
    breadth = width // sharp.shape[0]
    chips = lax.axis_size("tm") // 2
    block = x.shape
    part = (groups, breadth, HALF)
    x_odd = swap_with(x, "stations", lambda i: i + 2 * (i % 2) - 1)
    x_even = swap_with(x, "stations", lambda i: i ^ 1)
    wide = groups * T
    sums = (groups, patches, 2 * width)
    (means,) = call(means_kernel, breadth, [((HALF, HALF), BF16)], (), name="means", flops=10**10)
    k, v, keep, give = call(
        states_kernel, breadth, [(block, BF16)] * 2 + [(part, F32), (part, BF16)], (x, w, means), name="states"
    )
    got = swap_with(give, "tm", lambda i: i ^ 1)
    (total,) = call(combine_kernel, breadth, [(part, BF16)], (keep, got), name="combine")
    pieces = [swap_with(total, "tm", lambda i: i ^ (2 * m)) for m in range(chips - 1, 0, -1)]
    q, lin = call(
        own_kernel,
        breadth,
        [(block, BF16), (block, F32)],
        (x, w, means, k, v, total),
        name="own",
        through={5: None},
    )
    masks, rows = call(
        masks_kernel,
        breadth,
        [((3, wide, wide * PAIR // breadth), F32), ((width // PAIR, wide * PAIR // breadth), F32)],
        (table, tally.reshape(1, -1), sharp.reshape(1, -1), total),
        name="masks",
        through={3: None},
    )
    (acc,) = call(near_kernel, breadth, [(sums, F32)], (k, v, q, rows, masks), name="near")
    acc, keep = call(
        even_kernel,
        breadth,
        [(sums, F32), (part, F32)],
        (x_even, w, means, q, rows, masks, acc, keep),
        [(block, BF16)] * 2,
        name="even",
        through={7: 1},
    )
    k_odd, v_odd, keep = call(
        odd_keys_kernel,
        breadth,
        [(block, BF16)] * 2 + [(part, F32)],
        (x_odd, w, means, keep, close),
        name="keys",
        through={3: 2, 4: None},
    )
    send, mine = call(carry_kernel, breadth, [(part, BF16)] * 2, (keep, got, *pieces), name="carry")
    other = swap_with(send, "tm", lambda i: i ^ 1)
    (gathered,) = call(odd_kernel, breadth, [(block, BF16)], (k_odd, v_odd, q, rows, masks, acc), name="odd")
    (out,) = call(
        closing_kernel,
        breadth,
        [(block, BF16)],
        (q, lin, mine, other, means, close, x, gathered),
        [(block, BF16), pltpu.SemaphoreType.DMA((groups,))],
        name="closing",
        space=pl.ANY,
    )
    return out


def solution(mesh):
    return jax.shard_map(
        per_device,
        mesh=mesh,
        in_specs=(P("stations", "tm", None), P(), P(), P(), P("stations", None), P("stations")),
        out_specs=P("stations", "tm", None),
        check_vma=False,
    )
```

```python
import functools
import math

import jax
import jax.numpy as jnp
from jax import lax
from jax.experimental import pallas as pl
from jax.experimental.pallas import tpu as pltpu
from jax.sharding import PartitionSpec as P

NEAR = 4
HALF = 256
PAIR = 128
T = 32
F32 = jnp.float32
BF16 = jnp.bfloat16
VMEM = pltpu.VMEM


def dot(a, b):
    return jnp.dot(a, b, preferred_element_type=F32)


def dot_nt(a, b):
    return lax.dot_general(a, b, (((1,), (1,)), ((), ())), preferred_element_type=F32)


def dot_tn(a, b):
    return lax.dot_general(a, b, (((0,), (0,)), ((), ())), preferred_element_type=F32)


def row_norm(x):
    xf = x.astype(F32)
    return (xf * lax.rsqrt(jnp.mean(xf * xf, axis=-1, keepdims=True) + 1e-06)).astype(BF16)


def head_ids(shape, axis, breadth):
    return lax.broadcasted_iota(jnp.int32, shape, axis) // breadth


def means_kernel(breadth, means_ref):
    same = head_ids((HALF, HALF), 0, breadth) == head_ids((HALF, HALF), 1, breadth)
    means_ref[...] = jnp.where(same, 1.0 / breadth, 0.0).astype(BF16)


def head_norm(values, means, epsilon):
    square = (values * values).astype(BF16)
    return (values * lax.rsqrt(dot(square, means) + epsilon)).astype(BF16)


def exact_head_norm(values, means, epsilon):
    square = values * values
    high = square.astype(BF16)
    low = (square - high.astype(F32)).astype(BF16)
    return (values * lax.rsqrt(dot(high, means) + dot(low, means) + epsilon)).astype(BF16)


def own_head(values, j, breadth):
    ids = head_ids(values.shape, 1, breadth)
    return jnp.where(ids == j, values, jnp.zeros_like(values))


def pick(low, high, breadth):
    return jnp.where(head_ids(low.shape, 1, breadth) == 0, low, high)


def stack(values, breadth):
    return jnp.concatenate([own_head(values, j, breadth) for j in range(PAIR // breadth)], axis=0)


def cut(ref, c, u):
    groups = ref.shape[0]
    return ref[:, c * T : (c + 1) * T, u * PAIR : (u + 1) * PAIR].reshape(groups * T, PAIR)


def project(normed, w_ref, first, count):
    return [dot(normed, w_ref[:, first + h * HALF : first + (h + 1) * HALF]) for h in range(count)]


def keys_values(x_ref, w_ref, means_ref, k_ref, v_ref, breadth, norm=head_norm):
    groups, patches, width = x_ref.shape
    halves = width // HALF
    means = means_ref[...]
    normed = row_norm(x_ref[...].reshape(groups * patches, width))
    keys = project(normed, w_ref, width, halves)
    values = project(normed, w_ref, 2 * width, halves)
    for h in range(halves):
        at = slice(h * HALF, (h + 1) * HALF)
        v_ref[:, :, at] = values[h].astype(BF16).reshape(groups, patches, HALF)
        k_ref[:, :, at] = norm(keys[h], means, 1e-06).reshape(groups, patches, HALF)


def staggered(items, *stages):
    held = [{} for _ in stages]
    for i in range(len(items) + len(stages) - 1):
        for s, stage in enumerate(stages):
            if 0 <= i - s < len(items):
                before = (held[s - 1].pop(i - s),) if s else ()
                held[s][i - s] = stage(*before, *items[i - s])


def neighbours(breadth, q_ref, windows, row_ref, emit):
    groups, patches, width = q_ref.shape
    wide = groups * T
    ones = stack(jnp.ones((wide, PAIR), BF16), breadth)
    sums = {}

    def score(u, c, n):
        return dot_nt(cut(q_ref, c, u), stack(cut(windows[n][0], c, u), breadth))

    def share(scores, u, c, n):
        return (jnp.exp2(scores * row_ref[u : u + 1, :]) * windows[n][2][...]).astype(BF16)

    def gather(shares, u, c, n):
        spread = jnp.concatenate([stack(cut(windows[n][1], c, u), breadth), ones], axis=1)
        part = dot(shares, spread)
        total = sums.pop((u, c)) + part if n else part
        if n + 1 < len(windows):
            sums[(u, c)] = total
        else:
            emit(c, u, total)

    items = [(u, c, n) for u in range(width // PAIR) for c in range(patches // T) for n in range(len(windows))]
    staggered(items, score, share, gather)


def masks_kernel(breadth, table_ref, tally_ref, sharp_ref, total_ref, mask_ref, row_ref):
    groups, slots = table_ref.shape
    wide = groups * T
    heads = PAIR // breadth
    scale = math.log2(math.e) / math.sqrt(breadth)
    lane = lax.broadcasted_iota(jnp.int32, (1, heads * wide), 1) // wide
    for u in range(row_ref.shape[0]):
        row = jnp.zeros(lane.shape, F32)
        for j in range(heads):
            row = jnp.where(lane == j, sharp_ref[:, u * heads + j : u * heads + j + 1], row)
        row_ref[u : u + 1, :] = row * scale
    station = lax.axis_index("stations")
    around = (station, station ^ 1, station + 2 * (station % 2) - 1)
    position = lax.broadcasted_iota(jnp.int32, (1, wide), 1) // T
    ids = jnp.concatenate([place * groups + position for place in around], axis=1)
    rows = []
    for g in range(groups):
        counts = jnp.zeros(ids.shape, F32)
        for j in range(slots):
            slot = jnp.where(tally_ref[:, g : g + 1] > j, table_ref[g : g + 1, j : j + 1], -(1 << 20))
            counts += jnp.where(ids == slot, 1.0, 0.0)
        rows.append(counts)
    t_row = lax.broadcasted_iota(jnp.int32, (T, wide), 0)
    t_col = lax.broadcasted_iota(jnp.int32, (T, wide), 1) % T
    for n in range(len(around)):
        for g in range(groups):
            block = jnp.where(t_row == t_col, jnp.broadcast_to(rows[g][:, n * wide : (n + 1) * wide], (T, wide)), 0.0)
            for j in range(heads):
                mask_ref[n, g * T : (g + 1) * T, j * wide : (j + 1) * wide] = block


def states_kernel(breadth, x_ref, w_ref, means_ref, k_ref, v_ref, keep_ref, give_ref):
    groups, patches, width = x_ref.shape
    core = lax.axis_index("tm") % 2
    keys_values(x_ref, w_ref, means_ref, k_ref, v_ref, breadth, exact_head_norm)
    for h in range(width // HALF):
        states = []
        for g in range(groups):
            pairs = []
            for u in range(h * HALF // PAIR, (h + 1) * HALF // PAIR):
                at = slice(u * PAIR, (u + 1) * PAIR)
                full = dot_tn(k_ref[g, :, at], v_ref[g, :, at])
                pairs.append(pick(full[:breadth], full[breadth:], breadth))
            states.append(jnp.concatenate(pairs, axis=1))

        @pl.when(core == h)
        def _():
            for g in range(groups):
                keep_ref[g] = states[g]

        @pl.when(core != h)
        def _():
            for g in range(groups):
                give_ref[g] = states[g].astype(BF16)


def own_kernel(breadth, x_ref, w_ref, means_ref, k_ref, v_ref, total_ref, q_ref, lin_ref):
    groups, patches, width = x_ref.shape
    halves = width // HALF
    means = means_ref[...]
    wide = (patches, patches * (PAIR // breadth))
    causal = lax.broadcasted_iota(jnp.int32, wide, 0) >= lax.broadcasted_iota(jnp.int32, wide, 1) % patches
    queries = project(row_norm(x_ref[...].reshape(groups * patches, width)), w_ref, 0, halves)
    for h in range(halves):
        q = exact_head_norm(queries[h], means, 1e-06)
        q_ref[:, :, h * HALF : (h + 1) * HALF] = q.reshape(groups, patches, HALF)

    def score(h, g):
        scores = []
        for u in range(h * HALF // PAIR, (h + 1) * HALF // PAIR):
            at = slice(u * PAIR, (u + 1) * PAIR)
            scores.append(dot_nt(q_ref[g, :, at], stack(k_ref[g, :, at], breadth)))
        return scores

    def share(scores, h, g):
        return jnp.concatenate([jnp.where(causal, s, 0.0).astype(BF16) for s in scores], axis=1)

    def gather(shares, h, g):
        at = slice(h * HALF, (h + 1) * HALF)
        v = v_ref[g, :, at]
        spread = jnp.concatenate([own_head(v, j, breadth) for j in range(HALF // breadth)], axis=0)
        lin_ref[g, :, at] = dot(shares, spread)

    staggered([(h, g) for h in range(halves) for g in range(groups)], score, share, gather)


def near_kernel(breadth, k_ref, v_ref, q_ref, row_ref, mask_ref, acc_ref):
    groups = q_ref.shape[0]

    def emit(c, u, total):
        acc_ref[:, c * T : (c + 1) * T, u * 2 * PAIR : (u + 1) * 2 * PAIR] = total.reshape(groups, T, 2 * PAIR)

    neighbours(breadth, q_ref, [(k_ref, v_ref, mask_ref.at[0])], row_ref, emit)


def even_kernel(breadth, x_ref, w_ref, means_ref, q_ref, row_ref, mask_ref, acc_ref, keep_ref, sum_ref, kept_ref, k_ref, v_ref):
    groups = x_ref.shape[0]
    keys_values(x_ref, w_ref, means_ref, k_ref, v_ref, breadth)

    def emit(c, u, total):
        at = (slice(None), slice(c * T, (c + 1) * T), slice(u * 2 * PAIR, (u + 1) * 2 * PAIR))
        sum_ref[at] = acc_ref[at] + total.reshape(groups, T, 2 * PAIR)

    neighbours(breadth, q_ref, [(k_ref, v_ref, mask_ref.at[1])], row_ref, emit)


def odd_partner():
    station = lax.axis_index("stations")
    partner = station + 2 * (station % 2) - 1
    return (partner >= 0) & (partner < lax.axis_size("stations"))


def odd_keys_kernel(breadth, x_ref, w_ref, means_ref, keep_ref, close_ref, k_ref, v_ref, kept_ref):
    @pl.when(odd_partner())
    def _():
        keys_values(x_ref, w_ref, means_ref, k_ref, v_ref, breadth)


def odd_kernel(breadth, k_ref, v_ref, q_ref, row_ref, mask_ref, acc_ref, gathered_ref):
    groups, patches, width = q_ref.shape
    there = odd_partner()

    def part(c, u):
        return (slice(None), slice(c * T, (c + 1) * T), slice(u * 2 * PAIR, (u + 1) * 2 * PAIR))

    def finish(c, u, total):
        share, weight = total[:, :, :PAIR], total[:, :, PAIR:]
        near = pl.reciprocal(weight, approx=True)
        share = share * (near * (2.0 - weight * near))
        gathered_ref[:, c * T : (c + 1) * T, u * PAIR : (u + 1) * PAIR] = share.astype(BF16)

    @pl.when(there)
    def _():
        def emit(c, u, total):
            finish(c, u, acc_ref[part(c, u)] + total.reshape(groups, T, 2 * PAIR))

        neighbours(breadth, q_ref, [(k_ref, v_ref, mask_ref.at[2])], row_ref, emit)

    @pl.when(jnp.logical_not(there))
    def _():
        for u in range(width // PAIR):
            for c in range(patches // T):
                finish(c, u, acc_ref[part(c, u)])


def closing_kernel(breadth, q_ref, lin_ref, mine_ref, other_ref, means_ref, close_ref, x_ref, gathered_ref, out_hbm, out_ref, sem):
    groups, patches, width = q_ref.shape
    heads = HALF // breadth
    core = lax.axis_index("tm") % 2
    means = means_ref[...]
    copies = [pltpu.make_async_copy(out_ref.at[g], out_hbm.at[g], sem.at[g]) for g in range(groups)]

    def totals(g):
        both = []
        for h in range(width // HALF):
            at = slice(h * HALF, (h + 1) * HALF)
            state = jnp.where(core == h, mine_ref[g], other_ref[g])
            block = jnp.where(means > 0, jnp.concatenate([state] * heads, axis=0), jnp.zeros((), BF16))
            both.append(lin_ref[g, :, at] + dot(q_ref[g, :, at], block))
        return both

    def squares(both, g):
        return both, [dot((t * t).astype(BF16), means) for t in both]

    def normalize(pair, g):
        return [(t * lax.rsqrt(m + 1e-05)).astype(BF16) for t, m in zip(*pair)]

    def output(parts, g):
        mixed = dot(jnp.concatenate(parts + [gathered_ref[g]], axis=1), close_ref[...])
        out_ref[g] = (x_ref[g].astype(F32) + mixed).astype(BF16)
        copies[g].start()

    staggered([(g,) for g in range(groups)], totals, squares, normalize, output)
    for copy in copies:
        copy.wait()


def combine_kernel(breadth, keep_ref, got_ref, total_ref):
    total_ref[...] = (keep_ref[...] + got_ref[...].astype(F32)).astype(BF16)


def carry_kernel(breadth, keep_ref, got_ref, *refs):
    *pieces, send_ref, mine_ref = refs
    core, chip = lax.axis_index("tm") % 2, lax.axis_index("tm") // 2
    before = jnp.zeros(keep_ref.shape, F32)
    for m, piece in enumerate(pieces, 1):
        before += jnp.where((chip ^ m) < chip, piece[...].astype(F32), 0.0)
    send_ref[...] = (before + jnp.where(core == 0, keep_ref[...], 0.0)).astype(BF16)
    mine_ref[...] = (before + jnp.where(core == 0, 0.0, got_ref[...].astype(F32))).astype(BF16)


def call(kernel, breadth, outs, args, scratch=(), flops=10**6, name=None, through=None, space=VMEM):
    in_specs = [pl.BlockSpec(memory_space=VMEM) for _ in args]
    out_specs = [pl.BlockSpec(memory_space=space) for _ in outs]
    for i, o in (through or {}).items():
        in_specs[i] = pl.BlockSpec(memory_space=pl.ANY)
        if o is not None:
            out_specs[o] = in_specs[i]
    return pl.pallas_call(
        functools.partial(kernel, breadth),
        out_shape=[jax.ShapeDtypeStruct(s, d) for s, d in outs],
        in_specs=in_specs,
        out_specs=out_specs,
        scratch_shapes=[pltpu.VMEM(*s) if isinstance(s, tuple) else s for s in scratch],
        input_output_aliases={i: o for i, o in (through or {}).items() if o is not None},
        compiler_params=pltpu.CompilerParams(vmem_limit_bytes=10 * 2**20),
        cost_estimate=pl.CostEstimate(flops=flops, bytes_accessed=2**12, transcendentals=0),
        name=name,
    )(*args)


def swap_with(value, axis, partner):
    size = lax.axis_size(axis)
    pairs = [(i, partner(i)) for i in range(size) if 0 <= partner(i) < size]
    return lax.ppermute(value, axis, pairs)


def per_device(x, w, close, sharp, table, tally):
    groups, patches, width = x.shape
    breadth = width // sharp.shape[0]
    chips = lax.axis_size("tm") // 2
    block = x.shape
    part = (groups, breadth, HALF)
    x_odd = swap_with(x, "stations", lambda i: i + 2 * (i % 2) - 1)
    x_even = swap_with(x, "stations", lambda i: i ^ 1)
    wide = groups * T
    sums = (groups, patches, 2 * width)
    (means,) = call(means_kernel, breadth, [((HALF, HALF), BF16)], (), name="means", flops=10**10)
    k, v, keep, give = call(
        states_kernel, breadth, [(block, BF16)] * 2 + [(part, F32), (part, BF16)], (x, w, means), name="states"
    )
    got = swap_with(give, "tm", lambda i: i ^ 1)
    (total,) = call(combine_kernel, breadth, [(part, BF16)], (keep, got), name="combine")
    pieces = [swap_with(total, "tm", lambda i: i ^ (2 * m)) for m in range(1, chips)]
    q, lin = call(
        own_kernel,
        breadth,
        [(block, BF16), (block, F32)],
        (x, w, means, k, v, total),
        name="own",
        through={5: None},
    )
    masks, rows = call(
        masks_kernel,
        breadth,
        [((3, wide, wide * PAIR // breadth), F32), ((width // PAIR, wide * PAIR // breadth), F32)],
        (table, tally.reshape(1, -1), sharp.reshape(1, -1), total),
        name="masks",
        through={3: None},
    )
    (acc,) = call(near_kernel, breadth, [(sums, F32)], (k, v, q, rows, masks), name="near")
    acc, keep = call(
        even_kernel,
        breadth,
        [(sums, F32), (part, F32)],
        (x_even, w, means, q, rows, masks, acc, keep),
        [(block, BF16)] * 2,
        name="even",
        through={7: 1},
    )
    k_odd, v_odd, keep = call(
        odd_keys_kernel,
        breadth,
        [(block, BF16)] * 2 + [(part, F32)],
        (x_odd, w, means, keep, close),
        name="keys",
        through={3: 2, 4: None},
    )
    send, mine = call(carry_kernel, breadth, [(part, BF16)] * 2, (keep, got, *pieces), name="carry")
    other = swap_with(send, "tm", lambda i: i ^ 1)
    (gathered,) = call(odd_kernel, breadth, [(block, BF16)], (k_odd, v_odd, q, rows, masks, acc), name="odd")
    (out,) = call(
        closing_kernel,
        breadth,
        [(block, BF16)],
        (q, lin, mine, other, means, close, x, gathered),
        [(block, BF16), pltpu.SemaphoreType.DMA((groups,))],
        name="closing",
        space=pl.ANY,
    )
    return out


def solution(mesh):
    return jax.shard_map(
        per_device,
        mesh=mesh,
        in_specs=(P("stations", "tm", None), P(), P(), P(), P("stations", None), P("stations")),
        out_specs=P("stations", "tm", None),
        check_vma=False,
    )
```

```python
import functools
import math

import jax
import jax.numpy as jnp
from jax import lax
from jax.experimental import pallas as pl
from jax.experimental.pallas import tpu as pltpu
from jax.sharding import PartitionSpec as P

NEAR = 4
HALF = 256
PAIR = 128
T = 32
F32 = jnp.float32
BF16 = jnp.bfloat16
VMEM = pltpu.VMEM


def dot(a, b):
    return jnp.dot(a, b, preferred_element_type=F32)


def dot_nt(a, b):
    return lax.dot_general(a, b, (((1,), (1,)), ((), ())), preferred_element_type=F32)


def dot_tn(a, b):
    return lax.dot_general(a, b, (((0,), (0,)), ((), ())), preferred_element_type=F32)


def row_norm(x):
    xf = x.astype(F32)
    return (xf * lax.rsqrt(jnp.mean(xf * xf, axis=-1, keepdims=True) + 1e-06)).astype(BF16)


def head_ids(shape, axis, breadth):
    return lax.broadcasted_iota(jnp.int32, shape, axis) // breadth


def means_kernel(breadth, means_ref):
    same = head_ids((HALF, HALF), 0, breadth) == head_ids((HALF, HALF), 1, breadth)
    means_ref[...] = jnp.where(same, 1.0 / breadth, 0.0).astype(BF16)


def head_norm(values, means, epsilon):
    square = (values * values).astype(BF16)
    return (values * lax.rsqrt(dot(square, means) + epsilon)).astype(BF16)


def exact_head_norm(values, means, epsilon):
    square = values * values
    high = square.astype(BF16)
    low = (square - high.astype(F32)).astype(BF16)
    return (values * lax.rsqrt(dot(high, means) + dot(low, means) + epsilon)).astype(BF16)


def own_head(values, j, breadth):
    ids = head_ids(values.shape, 1, breadth)
    return jnp.where(ids == j, values, jnp.zeros_like(values))


def pick(low, high, breadth):
    return jnp.where(head_ids(low.shape, 1, breadth) == 0, low, high)


def stack(values, breadth):
    return jnp.concatenate([own_head(values, j, breadth) for j in range(PAIR // breadth)], axis=0)


def cut(ref, c, u):
    groups = ref.shape[0]
    return ref[:, c * T : (c + 1) * T, u * PAIR : (u + 1) * PAIR].reshape(groups * T, PAIR)


def project(normed, w_ref, first, count):
    return [dot(normed, w_ref[:, first + h * HALF : first + (h + 1) * HALF]) for h in range(count)]


def keys_values(x_ref, w_ref, means_ref, k_ref, v_ref, breadth, norm=head_norm):
    groups, patches, width = x_ref.shape
    halves = width // HALF
    means = means_ref[...]
    normed = row_norm(x_ref[...].reshape(groups * patches, width))
    keys = project(normed, w_ref, width, halves)
    values = project(normed, w_ref, 2 * width, halves)
    for h in range(halves):
        at = slice(h * HALF, (h + 1) * HALF)
        v_ref[:, :, at] = values[h].astype(BF16).reshape(groups, patches, HALF)
        k_ref[:, :, at] = norm(keys[h], means, 1e-06).reshape(groups, patches, HALF)


def staggered(items, *stages):
    held = [{} for _ in stages]
    for i in range(len(items) + len(stages) - 1):
        for s, stage in enumerate(stages):
            if 0 <= i - s < len(items):
                before = (held[s - 1].pop(i - s),) if s else ()
                held[s][i - s] = stage(*before, *items[i - s])


def neighbours(breadth, q_ref, windows, row_ref, emit):
    groups, patches, width = q_ref.shape
    wide = groups * T
    ones = stack(jnp.ones((wide, PAIR), BF16), breadth)
    sums = {}

    def score(u, c, n):
        return dot_nt(cut(q_ref, c, u), stack(cut(windows[n][0], c, u), breadth))

    def share(scores, u, c, n):
        return (jnp.exp2(scores * row_ref[u : u + 1, :]) * windows[n][2][...]).astype(BF16)

    def gather(shares, u, c, n):
        spread = jnp.concatenate([stack(cut(windows[n][1], c, u), breadth), ones], axis=1)
        part = dot(shares, spread)
        total = sums.pop((u, c)) + part if n else part
        if n + 1 < len(windows):
            sums[(u, c)] = total
        else:
            emit(c, u, total)

    items = [(u, c, n) for u in range(width // PAIR) for c in range(patches // T) for n in range(len(windows))]
    staggered(items, score, share, gather)


def masks_kernel(breadth, table_ref, tally_ref, sharp_ref, total_ref, mask_ref, row_ref):
    groups, slots = table_ref.shape
    wide = groups * T
    heads = PAIR // breadth
    scale = math.log2(math.e) / math.sqrt(breadth)
    lane = lax.broadcasted_iota(jnp.int32, (1, heads * wide), 1) // wide
    for u in range(row_ref.shape[0]):
        row = jnp.zeros(lane.shape, F32)
        for j in range(heads):
            row = jnp.where(lane == j, sharp_ref[:, u * heads + j : u * heads + j + 1], row)
        row_ref[u : u + 1, :] = row * scale
    station = lax.axis_index("stations")
    around = (station, station ^ 1, station + 2 * (station % 2) - 1)
    position = lax.broadcasted_iota(jnp.int32, (1, wide), 1) // T
    ids = jnp.concatenate([place * groups + position for place in around], axis=1)
    rows = []
    for g in range(groups):
        counts = jnp.zeros(ids.shape, F32)
        for j in range(slots):
            slot = jnp.where(tally_ref[:, g : g + 1] > j, table_ref[g : g + 1, j : j + 1], -(1 << 20))
            counts += jnp.where(ids == slot, 1.0, 0.0)
        rows.append(counts)
    t_row = lax.broadcasted_iota(jnp.int32, (T, wide), 0)
    t_col = lax.broadcasted_iota(jnp.int32, (T, wide), 1) % T
    for n in range(len(around)):
        for g in range(groups):
            block = jnp.where(t_row == t_col, jnp.broadcast_to(rows[g][:, n * wide : (n + 1) * wide], (T, wide)), 0.0)
            for j in range(heads):
                mask_ref[n, g * T : (g + 1) * T, j * wide : (j + 1) * wide] = block


def states_kernel(breadth, x_ref, w_ref, means_ref, k_ref, v_ref, keep_ref, give_ref):
    groups, patches, width = x_ref.shape
    core = lax.axis_index("tm") % 2
    keys_values(x_ref, w_ref, means_ref, k_ref, v_ref, breadth, exact_head_norm)
    for h in range(width // HALF):
        states = []
        for g in range(groups):
            pairs = []
            for u in range(h * HALF // PAIR, (h + 1) * HALF // PAIR):
                at = slice(u * PAIR, (u + 1) * PAIR)
                full = dot_tn(k_ref[g, :, at], v_ref[g, :, at])
                pairs.append(pick(full[:breadth], full[breadth:], breadth))
            states.append(jnp.concatenate(pairs, axis=1))

        @pl.when(core == h)
        def _():
            for g in range(groups):
                keep_ref[g] = states[g]

        @pl.when(core != h)
        def _():
            for g in range(groups):
                give_ref[g] = states[g].astype(BF16)


def own_kernel(breadth, x_ref, w_ref, means_ref, k_ref, v_ref, total_ref, q_ref, lin_ref):
    groups, patches, width = x_ref.shape
    halves = width // HALF
    means = means_ref[...]
    wide = (patches, patches * (PAIR // breadth))
    causal = lax.broadcasted_iota(jnp.int32, wide, 0) >= lax.broadcasted_iota(jnp.int32, wide, 1) % patches
    queries = project(row_norm(x_ref[...].reshape(groups * patches, width)), w_ref, 0, halves)
    for h in range(halves):
        q = exact_head_norm(queries[h], means, 1e-06)
        q_ref[:, :, h * HALF : (h + 1) * HALF] = q.reshape(groups, patches, HALF)

    def score(h, g):
        scores = []
        for u in range(h * HALF // PAIR, (h + 1) * HALF // PAIR):
            at = slice(u * PAIR, (u + 1) * PAIR)
            scores.append(dot_nt(q_ref[g, :, at], stack(k_ref[g, :, at], breadth)))
        return scores

    def share(scores, h, g):
        return jnp.concatenate([jnp.where(causal, s, 0.0).astype(BF16) for s in scores], axis=1)

    def gather(shares, h, g):
        at = slice(h * HALF, (h + 1) * HALF)
        v = v_ref[g, :, at]
        spread = jnp.concatenate([own_head(v, j, breadth) for j in range(HALF // breadth)], axis=0)
        lin_ref[g, :, at] = dot(shares, spread)

    staggered([(h, g) for h in range(halves) for g in range(groups)], score, share, gather)


def near_kernel(breadth, k_ref, v_ref, q_ref, row_ref, mask_ref, acc_ref):
    groups = q_ref.shape[0]

    def emit(c, u, total):
        acc_ref[:, c * T : (c + 1) * T, u * 2 * PAIR : (u + 1) * 2 * PAIR] = total.reshape(groups, T, 2 * PAIR)

    neighbours(breadth, q_ref, [(k_ref, v_ref, mask_ref.at[0])], row_ref, emit)


def odd_partner():
    station = lax.axis_index("stations")
    partner = station + 2 * (station % 2) - 1
    return (partner >= 0) & (partner < lax.axis_size("stations"))


def odd_keys_kernel(breadth, x_ref, w_ref, means_ref, keep_ref, close_ref, acc_ref, k_ref, v_ref, kept_ref):
    @pl.when(odd_partner())
    def _():
        keys_values(x_ref, w_ref, means_ref, k_ref, v_ref, breadth)


def even_keys_kernel(breadth, x_ref, w_ref, means_ref, mine_ref, k_ref, v_ref):
    keys_values(x_ref, w_ref, means_ref, k_ref, v_ref, breadth)


def halo_kernel(breadth, ke_ref, ve_ref, ko_ref, vo_ref, q_ref, row_ref, mask_ref, acc_ref, gathered_ref):
    groups = q_ref.shape[0]
    even = (ke_ref, ve_ref, mask_ref.at[1])
    odd = (ko_ref, vo_ref, mask_ref.at[2])

    def emit(c, u, total):
        span = slice(c * T, (c + 1) * T)
        total = acc_ref[:, span, u * 2 * PAIR : (u + 1) * 2 * PAIR] + total.reshape(groups, T, 2 * PAIR)
        share, weight = total[:, :, :PAIR], total[:, :, PAIR:]
        near = pl.reciprocal(weight, approx=True)
        share = share * (near * (2.0 - weight * near))
        gathered_ref[:, span, u * PAIR : (u + 1) * PAIR] = share.astype(BF16)

    @pl.when(odd_partner())
    def _():
        neighbours(breadth, q_ref, [even, odd], row_ref, emit)

    @pl.when(jnp.logical_not(odd_partner()))
    def _():
        neighbours(breadth, q_ref, [even], row_ref, emit)


def closing_kernel(breadth, q_ref, lin_ref, mine_ref, other_ref, means_ref, close_ref, x_ref, gathered_ref, out_hbm, out_ref, sem):
    groups, patches, width = q_ref.shape
    heads = HALF // breadth
    core = lax.axis_index("tm") % 2
    means = means_ref[...]
    copies = [pltpu.make_async_copy(out_ref.at[g], out_hbm.at[g], sem.at[g]) for g in range(groups)]

    def totals(g):
        both = []
        for h in range(width // HALF):
            at = slice(h * HALF, (h + 1) * HALF)
            state = jnp.where(core == h, mine_ref[g], other_ref[g])
            block = jnp.where(means > 0, jnp.concatenate([state] * heads, axis=0), jnp.zeros((), BF16))
            both.append(lin_ref[g, :, at] + dot(q_ref[g, :, at], block))
        return both

    def squares(both, g):
        return both, [dot((t * t).astype(BF16), means) for t in both]

    def normalize(pair, g):
        return [(t * lax.rsqrt(m + 1e-05)).astype(BF16) for t, m in zip(*pair)]

    def output(parts, g):
        mixed = dot(jnp.concatenate(parts + [gathered_ref[g]], axis=1), close_ref[...])
        out_ref[g] = (x_ref[g].astype(F32) + mixed).astype(BF16)
        copies[g].start()

    staggered([(g,) for g in range(groups)], totals, squares, normalize, output)
    for copy in copies:
        copy.wait()


def combine_kernel(breadth, keep_ref, got_ref, total_ref):
    total_ref[...] = (keep_ref[...] + got_ref[...].astype(F32)).astype(BF16)


def carry_kernel(breadth, keep_ref, got_ref, *refs):
    *pieces, send_ref, mine_ref = refs
    core, chip = lax.axis_index("tm") % 2, lax.axis_index("tm") // 2
    before = jnp.zeros(keep_ref.shape, F32)
    for m, piece in enumerate(pieces, 1):
        before += jnp.where((chip ^ m) < chip, piece[...].astype(F32), 0.0)
    send_ref[...] = (before + jnp.where(core == 0, keep_ref[...], 0.0)).astype(BF16)
    mine_ref[...] = (before + jnp.where(core == 0, 0.0, got_ref[...].astype(F32))).astype(BF16)


def call(kernel, breadth, outs, args, scratch=(), flops=10**6, name=None, through=None, space=VMEM):
    in_specs = [pl.BlockSpec(memory_space=VMEM) for _ in args]
    out_specs = [pl.BlockSpec(memory_space=space) for _ in outs]
    for i, o in (through or {}).items():
        in_specs[i] = pl.BlockSpec(memory_space=pl.ANY)
        if o is not None:
            out_specs[o] = in_specs[i]
    return pl.pallas_call(
        functools.partial(kernel, breadth),
        out_shape=[jax.ShapeDtypeStruct(s, d) for s, d in outs],
        in_specs=in_specs,
        out_specs=out_specs,
        scratch_shapes=[pltpu.VMEM(*s) if isinstance(s, tuple) else s for s in scratch],
        input_output_aliases={i: o for i, o in (through or {}).items() if o is not None},
        compiler_params=pltpu.CompilerParams(vmem_limit_bytes=10 * 2**20),
        cost_estimate=pl.CostEstimate(flops=flops, bytes_accessed=2**12, transcendentals=0),
        name=name,
    )(*args)


def swap_with(value, axis, partner):
    size = lax.axis_size(axis)
    pairs = [(i, partner(i)) for i in range(size) if 0 <= partner(i) < size]
    return lax.ppermute(value, axis, pairs)


def per_device(x, w, close, sharp, table, tally):
    groups, patches, width = x.shape
    breadth = width // sharp.shape[0]
    chips = lax.axis_size("tm") // 2
    block = x.shape
    part = (groups, breadth, HALF)
    x_odd = swap_with(x, "stations", lambda i: i + 2 * (i % 2) - 1)
    x_even = swap_with(x, "stations", lambda i: i ^ 1)
    wide = groups * T
    sums = (groups, patches, 2 * width)
    (means,) = call(means_kernel, breadth, [((HALF, HALF), BF16)], (), name="means", flops=10**10)
    k, v, keep, give = call(
        states_kernel, breadth, [(block, BF16)] * 2 + [(part, F32), (part, BF16)], (x, w, means), name="states"
    )
    got = swap_with(give, "tm", lambda i: i ^ 1)
    (total,) = call(combine_kernel, breadth, [(part, BF16)], (keep, got), name="combine")
    pieces = [swap_with(total, "tm", lambda i: i ^ (2 * m)) for m in range(1, chips)]
    q, lin = call(
        own_kernel,
        breadth,
        [(block, BF16), (block, F32)],
        (x, w, means, k, v, total),
        name="own",
        through={5: None},
    )
    masks, rows = call(
        masks_kernel,
        breadth,
        [((3, wide, wide * PAIR // breadth), F32), ((width // PAIR, wide * PAIR // breadth), F32)],
        (table, tally.reshape(1, -1), sharp.reshape(1, -1), total),
        name="masks",
        through={3: None},
    )
    (acc,) = call(near_kernel, breadth, [(sums, F32)], (k, v, q, rows, masks), name="near")
    k_odd, v_odd, keep = call(
        odd_keys_kernel,
        breadth,
        [(block, BF16)] * 2 + [(part, F32)],
        (x_odd, w, means, keep, close, acc),
        name="odd",
        through={3: 2, 4: None, 5: None},
    )
    send, mine = call(carry_kernel, breadth, [(part, BF16)] * 2, (keep, got, *pieces), name="carry")
    other = swap_with(send, "tm", lambda i: i ^ 1)
    k_even, v_even = call(
        even_keys_kernel,
        breadth,
        [(block, BF16)] * 2,
        (x_even, w, means, mine),
        name="even",
        through={3: None},
    )
    (gathered,) = call(
        halo_kernel, breadth, [(block, BF16)], (k_even, v_even, k_odd, v_odd, q, rows, masks, acc), name="halo"
    )
    (out,) = call(
        closing_kernel,
        breadth,
        [(block, BF16)],
        (q, lin, mine, other, means, close, x, gathered),
        [(block, BF16), pltpu.SemaphoreType.DMA((groups,))],
        name="closing",
        space=pl.ANY,
    )
    return out


def solution(mesh):
    return jax.shard_map(
        per_device,
        mesh=mesh,
        in_specs=(P("stations", "tm", None), P(), P(), P(), P("stations", None), P("stations")),
        out_specs=P("stations", "tm", None),
        check_vma=False,
    )
```

```python
import functools
import math

import jax
import jax.numpy as jnp
from jax import lax
from jax.experimental import pallas as pl
from jax.experimental.pallas import tpu as pltpu
from jax.sharding import PartitionSpec as P

NEAR = 4
HALF = 256
PAIR = 128
T = 32
F32 = jnp.float32
BF16 = jnp.bfloat16
VMEM = pltpu.VMEM


def dot(a, b):
    return jnp.dot(a, b, preferred_element_type=F32)


def dot_nt(a, b):
    return lax.dot_general(a, b, (((1,), (1,)), ((), ())), preferred_element_type=F32)


def dot_tn(a, b):
    return lax.dot_general(a, b, (((0,), (0,)), ((), ())), preferred_element_type=F32)


def row_norm(x):
    xf = x.astype(F32)
    return (xf * lax.rsqrt(jnp.mean(xf * xf, axis=-1, keepdims=True) + 1e-06)).astype(BF16)


def row_scale(x):
    xf = x.astype(F32)
    return lax.rsqrt(jnp.mean(xf * xf, axis=-1, keepdims=True) + 1e-06)


def head_ids(shape, axis, breadth):
    return lax.broadcasted_iota(jnp.int32, shape, axis) // breadth


def means_kernel(breadth, means_ref):
    same = head_ids((HALF, HALF), 0, breadth) == head_ids((HALF, HALF), 1, breadth)
    means_ref[...] = jnp.where(same, 1.0 / breadth, 0.0).astype(BF16)


def head_norm(values, means, epsilon):
    square = (values * values).astype(BF16)
    return (values * lax.rsqrt(dot(square, means) + epsilon)).astype(BF16)


def exact_head_norm(values, means, epsilon):
    square = values * values
    high = square.astype(BF16)
    low = (square - high.astype(F32)).astype(BF16)
    return (values * lax.rsqrt(dot(high, means) + dot(low, means) + epsilon)).astype(BF16)


def own_head(values, j, breadth):
    ids = head_ids(values.shape, 1, breadth)
    return jnp.where(ids == j, values, jnp.zeros_like(values))


def pick(low, high, breadth):
    return jnp.where(head_ids(low.shape, 1, breadth) == 0, low, high)


def stack(values, breadth):
    return jnp.concatenate([own_head(values, j, breadth) for j in range(PAIR // breadth)], axis=0)


def cut(ref, c, u):
    groups = ref.shape[0]
    return ref[:, c * T : (c + 1) * T, u * PAIR : (u + 1) * PAIR].reshape(groups * T, PAIR)


def project(normed, w_ref, first, count):
    return [dot(normed, w_ref[:, first + h * HALF : first + (h + 1) * HALF]) for h in range(count)]


def keys_values(x_ref, w_ref, means_ref, k_ref, v_ref, breadth, norm=head_norm):
    groups, patches, width = x_ref.shape
    halves = width // HALF
    means = means_ref[...]
    normed = row_norm(x_ref[...].reshape(groups * patches, width))
    keys = project(normed, w_ref, width, halves)
    values = project(normed, w_ref, 2 * width, halves)
    for h in range(halves):
        at = slice(h * HALF, (h + 1) * HALF)
        v_ref[:, :, at] = values[h].astype(BF16).reshape(groups, patches, HALF)
        k_ref[:, :, at] = norm(keys[h], means, 1e-06).reshape(groups, patches, HALF)


def halo_keys_values(x_ref, w_ref, means_ref, k_ref, v_ref, breadth):
    groups, patches, width = x_ref.shape
    halves = width // HALF
    means = means_ref[...]
    rows = x_ref[...].reshape(groups * patches, width)
    keys = project(rows, w_ref, width, halves)
    values = project(rows, w_ref, 2 * width, halves)
    scale = row_scale(rows)
    for h in range(halves):
        at = slice(h * HALF, (h + 1) * HALF)
        v_ref[:, :, at] = (values[h] * scale).astype(BF16).reshape(groups, patches, HALF)
        k_ref[:, :, at] = head_norm(keys[h] * scale, means, 1e-06).reshape(groups, patches, HALF)


def staggered(items, *stages):
    held = [{} for _ in stages]
    for i in range(len(items) + len(stages) - 1):
        for s, stage in enumerate(stages):
            if 0 <= i - s < len(items):
                before = (held[s - 1].pop(i - s),) if s else ()
                held[s][i - s] = stage(*before, *items[i - s])


def neighbours(breadth, q_ref, windows, row_ref, emit):
    groups, patches, width = q_ref.shape
    wide = groups * T
    ones = stack(jnp.ones((wide, PAIR), BF16), breadth)
    sums = {}

    def score(u, c, n):
        return dot_nt(cut(q_ref, c, u), stack(cut(windows[n][0], c, u), breadth))

    def share(scores, u, c, n):
        return (jnp.exp2(scores * row_ref[u : u + 1, :]) * windows[n][2][...]).astype(BF16)

    def gather(shares, u, c, n):
        spread = jnp.concatenate([stack(cut(windows[n][1], c, u), breadth), ones], axis=1)
        part = dot(shares, spread)
        total = sums.pop((u, c)) + part if n else part
        if n + 1 < len(windows):
            sums[(u, c)] = total
        else:
            emit(c, u, total)

    items = [(u, c, n) for u in range(width // PAIR) for c in range(patches // T) for n in range(len(windows))]
    staggered(items, score, share, gather)


def masks_kernel(breadth, table_ref, tally_ref, sharp_ref, total_ref, mask_ref, row_ref):
    groups, slots = table_ref.shape
    wide = groups * T
    heads = PAIR // breadth
    scale = math.log2(math.e) / math.sqrt(breadth)
    lane = lax.broadcasted_iota(jnp.int32, (1, heads * wide), 1) // wide
    for u in range(row_ref.shape[0]):
        row = jnp.zeros(lane.shape, F32)
        for j in range(heads):
            row = jnp.where(lane == j, sharp_ref[:, u * heads + j : u * heads + j + 1], row)
        row_ref[u : u + 1, :] = row * scale
    station = lax.axis_index("stations")
    around = (station, station ^ 1, station + 2 * (station % 2) - 1)
    position = lax.broadcasted_iota(jnp.int32, (1, wide), 1) // T
    ids = jnp.concatenate([place * groups + position for place in around], axis=1)
    rows = []
    for g in range(groups):
        counts = jnp.zeros(ids.shape, F32)
        for j in range(slots):
            slot = jnp.where(tally_ref[:, g : g + 1] > j, table_ref[g : g + 1, j : j + 1], -(1 << 20))
            counts += jnp.where(ids == slot, 1.0, 0.0)
        rows.append(counts)
    t_row = lax.broadcasted_iota(jnp.int32, (T, wide), 0)
    t_col = lax.broadcasted_iota(jnp.int32, (T, wide), 1) % T
    for n in range(len(around)):
        for g in range(groups):
            block = jnp.where(t_row == t_col, jnp.broadcast_to(rows[g][:, n * wide : (n + 1) * wide], (T, wide)), 0.0)
            for j in range(heads):
                mask_ref[n, g * T : (g + 1) * T, j * wide : (j + 1) * wide] = block


def states_kernel(breadth, x_ref, w_ref, means_ref, k_ref, v_ref, keep_ref, give_ref):
    groups, patches, width = x_ref.shape
    core = lax.axis_index("tm") % 2
    keys_values(x_ref, w_ref, means_ref, k_ref, v_ref, breadth, exact_head_norm)
    for h in range(width // HALF):
        states = []
        for g in range(groups):
            pairs = []
            for u in range(h * HALF // PAIR, (h + 1) * HALF // PAIR):
                at = slice(u * PAIR, (u + 1) * PAIR)
                full = dot_tn(k_ref[g, :, at], v_ref[g, :, at])
                pairs.append(pick(full[:breadth], full[breadth:], breadth))
            states.append(jnp.concatenate(pairs, axis=1))

        @pl.when(core == h)
        def _():
            for g in range(groups):
                keep_ref[g] = states[g]

        @pl.when(core != h)
        def _():
            for g in range(groups):
                give_ref[g] = states[g].astype(BF16)


def own_kernel(breadth, x_ref, w_ref, means_ref, k_ref, v_ref, total_ref, q_ref, lin_ref):
    groups, patches, width = x_ref.shape
    halves = width // HALF
    means = means_ref[...]
    wide = (patches, patches * (PAIR // breadth))
    causal = lax.broadcasted_iota(jnp.int32, wide, 0) >= lax.broadcasted_iota(jnp.int32, wide, 1) % patches
    queries = project(row_norm(x_ref[...].reshape(groups * patches, width)), w_ref, 0, halves)
    for h in range(halves):
        q = exact_head_norm(queries[h], means, 1e-06)
        q_ref[:, :, h * HALF : (h + 1) * HALF] = q.reshape(groups, patches, HALF)

    def score(h, g):
        scores = []
        for u in range(h * HALF // PAIR, (h + 1) * HALF // PAIR):
            at = slice(u * PAIR, (u + 1) * PAIR)
            scores.append(dot_nt(q_ref[g, :, at], stack(k_ref[g, :, at], breadth)))
        return scores

    def share(scores, h, g):
        return jnp.concatenate([jnp.where(causal, s, 0.0).astype(BF16) for s in scores], axis=1)

    def gather(shares, h, g):
        at = slice(h * HALF, (h + 1) * HALF)
        v = v_ref[g, :, at]
        spread = jnp.concatenate([own_head(v, j, breadth) for j in range(HALF // breadth)], axis=0)
        lin_ref[g, :, at] = dot(shares, spread)

    staggered([(h, g) for h in range(halves) for g in range(groups)], score, share, gather)


def near_kernel(breadth, k_ref, v_ref, q_ref, row_ref, mask_ref, acc_ref):
    groups = q_ref.shape[0]

    def emit(c, u, total):
        acc_ref[:, c * T : (c + 1) * T, u * 2 * PAIR : (u + 1) * 2 * PAIR] = total.reshape(groups, T, 2 * PAIR)

    neighbours(breadth, q_ref, [(k_ref, v_ref, mask_ref.at[0])], row_ref, emit)


def even_kernel(breadth, x_ref, w_ref, means_ref, q_ref, row_ref, mask_ref, acc_ref, keep_ref, sum_ref, kept_ref, k_ref, v_ref):
    groups = x_ref.shape[0]
    halo_keys_values(x_ref, w_ref, means_ref, k_ref, v_ref, breadth)

    def emit(c, u, total):
        at = (slice(None), slice(c * T, (c + 1) * T), slice(u * 2 * PAIR, (u + 1) * 2 * PAIR))
        sum_ref[at] = acc_ref[at] + total.reshape(groups, T, 2 * PAIR)

    neighbours(breadth, q_ref, [(k_ref, v_ref, mask_ref.at[1])], row_ref, emit)


def odd_partner():
    station = lax.axis_index("stations")
    partner = station + 2 * (station % 2) - 1
    return (partner >= 0) & (partner < lax.axis_size("stations"))


def odd_keys_kernel(breadth, x_ref, w_ref, means_ref, keep_ref, close_ref, k_ref, v_ref, kept_ref):
    @pl.when(odd_partner())
    def _():
        halo_keys_values(x_ref, w_ref, means_ref, k_ref, v_ref, breadth)


def odd_kernel(breadth, k_ref, v_ref, q_ref, row_ref, mask_ref, acc_ref, gathered_ref):
    groups, patches, width = q_ref.shape
    there = odd_partner()

    def part(c, u):
        return (slice(None), slice(c * T, (c + 1) * T), slice(u * 2 * PAIR, (u + 1) * 2 * PAIR))

    def finish(c, u, total):
        share, weight = total[:, :, :PAIR], total[:, :, PAIR:]
        near = pl.reciprocal(weight, approx=True)
        share = share * (near * (2.0 - weight * near))
        gathered_ref[:, c * T : (c + 1) * T, u * PAIR : (u + 1) * PAIR] = share.astype(BF16)

    @pl.when(there)
    def _():
        def emit(c, u, total):
            finish(c, u, acc_ref[part(c, u)] + total.reshape(groups, T, 2 * PAIR))

        neighbours(breadth, q_ref, [(k_ref, v_ref, mask_ref.at[2])], row_ref, emit)

    @pl.when(jnp.logical_not(there))
    def _():
        for u in range(width // PAIR):
            for c in range(patches // T):
                finish(c, u, acc_ref[part(c, u)])


def closing_kernel(breadth, q_ref, lin_ref, mine_ref, other_ref, means_ref, close_ref, x_ref, gathered_ref, out_hbm, out_ref, sem):
    groups, patches, width = q_ref.shape
    heads = HALF // breadth
    core = lax.axis_index("tm") % 2
    means = means_ref[...]
    copies = [pltpu.make_async_copy(out_ref.at[g], out_hbm.at[g], sem.at[g]) for g in range(groups)]

    def totals(g):
        both = []
        for h in range(width // HALF):
            at = slice(h * HALF, (h + 1) * HALF)
            state = jnp.where(core == h, mine_ref[g], other_ref[g])
            block = jnp.where(means > 0, jnp.concatenate([state] * heads, axis=0), jnp.zeros((), BF16))
            both.append(lin_ref[g, :, at] + dot(q_ref[g, :, at], block))
        return both

    def squares(both, g):
        return both, [dot((t * t).astype(BF16), means) for t in both]

    def normalize(pair, g):
        return [(t * lax.rsqrt(m + 1e-05)).astype(BF16) for t, m in zip(*pair)]

    def output(parts, g):
        mixed = dot(jnp.concatenate(parts + [gathered_ref[g]], axis=1), close_ref[...])
        out_ref[g] = (x_ref[g].astype(F32) + mixed).astype(BF16)
        copies[g].start()

    staggered([(g,) for g in range(groups)], totals, squares, normalize, output)
    for copy in copies:
        copy.wait()


def combine_kernel(breadth, keep_ref, got_ref, total_ref):
    total_ref[...] = (keep_ref[...] + got_ref[...].astype(F32)).astype(BF16)


def carry_kernel(breadth, keep_ref, got_ref, *refs):
    *pieces, send_ref, mine_ref = refs
    core, chip = lax.axis_index("tm") % 2, lax.axis_index("tm") // 2
    before = jnp.zeros(keep_ref.shape, F32)
    for m, piece in enumerate(pieces, 1):
        before += jnp.where((chip ^ m) < chip, piece[...].astype(F32), 0.0)
    send_ref[...] = (before + jnp.where(core == 0, keep_ref[...], 0.0)).astype(BF16)
    mine_ref[...] = (before + jnp.where(core == 0, 0.0, got_ref[...].astype(F32))).astype(BF16)


def call(kernel, breadth, outs, args, scratch=(), flops=10**6, name=None, through=None, space=VMEM):
    in_specs = [pl.BlockSpec(memory_space=VMEM) for _ in args]
    out_specs = [pl.BlockSpec(memory_space=space) for _ in outs]
    for i, o in (through or {}).items():
        in_specs[i] = pl.BlockSpec(memory_space=pl.ANY)
        if o is not None:
            out_specs[o] = in_specs[i]
    return pl.pallas_call(
        functools.partial(kernel, breadth),
        out_shape=[jax.ShapeDtypeStruct(s, d) for s, d in outs],
        in_specs=in_specs,
        out_specs=out_specs,
        scratch_shapes=[pltpu.VMEM(*s) if isinstance(s, tuple) else s for s in scratch],
        input_output_aliases={i: o for i, o in (through or {}).items() if o is not None},
        compiler_params=pltpu.CompilerParams(vmem_limit_bytes=10 * 2**20),
        cost_estimate=pl.CostEstimate(flops=flops, bytes_accessed=2**12, transcendentals=0),
        name=name,
    )(*args)


def swap_with(value, axis, partner):
    size = lax.axis_size(axis)
    pairs = [(i, partner(i)) for i in range(size) if 0 <= partner(i) < size]
    return lax.ppermute(value, axis, pairs)


def per_device(x, w, close, sharp, table, tally):
    groups, patches, width = x.shape
    breadth = width // sharp.shape[0]
    chips = lax.axis_size("tm") // 2
    block = x.shape
    part = (groups, breadth, HALF)
    x_odd = swap_with(x, "stations", lambda i: i + 2 * (i % 2) - 1)
    x_even = swap_with(x, "stations", lambda i: i ^ 1)
    wide = groups * T
    sums = (groups, patches, 2 * width)
    (means,) = call(means_kernel, breadth, [((HALF, HALF), BF16)], (), name="means", flops=10**10)
    k, v, keep, give = call(
        states_kernel, breadth, [(block, BF16)] * 2 + [(part, F32), (part, BF16)], (x, w, means), name="states"
    )
    got = swap_with(give, "tm", lambda i: i ^ 1)
    (total,) = call(combine_kernel, breadth, [(part, BF16)], (keep, got), name="combine")
    pieces = [swap_with(total, "tm", lambda i: i ^ (2 * m)) for m in range(1, chips)]
    q, lin = call(
        own_kernel,
        breadth,
        [(block, BF16), (block, F32)],
        (x, w, means, k, v, total),
        name="own",
        through={5: None},
    )
    masks, rows = call(
        masks_kernel,
        breadth,
        [((3, wide, wide * PAIR // breadth), F32), ((width // PAIR, wide * PAIR // breadth), F32)],
        (table, tally.reshape(1, -1), sharp.reshape(1, -1), total),
        name="masks",
        through={3: None},
    )
    (acc,) = call(near_kernel, breadth, [(sums, F32)], (k, v, q, rows, masks), name="near")
    acc, keep = call(
        even_kernel,
        breadth,
        [(sums, F32), (part, F32)],
        (x_even, w, means, q, rows, masks, acc, keep),
        [(block, BF16)] * 2,
        name="even",
        through={7: 1},
    )
    k_odd, v_odd, keep = call(
        odd_keys_kernel,
        breadth,
        [(block, BF16)] * 2 + [(part, F32)],
        (x_odd, w, means, keep, close),
        name="keys",
        through={3: 2, 4: None},
    )
    send, mine = call(carry_kernel, breadth, [(part, BF16)] * 2, (keep, got, *pieces), name="carry")
    other = swap_with(send, "tm", lambda i: i ^ 1)
    (gathered,) = call(odd_kernel, breadth, [(block, BF16)], (k_odd, v_odd, q, rows, masks, acc), name="odd")
    (out,) = call(
        closing_kernel,
        breadth,
        [(block, BF16)],
        (q, lin, mine, other, means, close, x, gathered),
        [(block, BF16), pltpu.SemaphoreType.DMA((groups,))],
        name="closing",
        space=pl.ANY,
    )
    return out


def solution(mesh):
    return jax.shard_map(
        per_device,
        mesh=mesh,
        in_specs=(P("stations", "tm", None), P(), P(), P(), P("stations", None), P("stations")),
        out_specs=P("stations", "tm", None),
        check_vma=False,
    )
```
